32 devices in a mesh: head: 8 (over y, x, core), ctx: 4 (over z).
Axes of the slice: x: 2, y: 2, z: 4, core: 2. Of those that a mesh axis runs over, the one named last changes fastest.
Arguments:
- queries: bfloat16 [8192, 2048], P(('ctx', 'head')), may hold values from -6 to 6
- keys: bfloat16 [8192, 2048], P(('ctx', 'head')), may hold values from -6 to 6
- values: bfloat16 [8192, 2048], P(('ctx', 'head')), may hold values from -24 to 24
- picks: int32 [16, 2], replicated, may hold values from 0 to 15, as said below
Outputs:
- attended: bfloat16 [8192, 2048], P(('ctx', 'head'))
The draws below stay inside these ranges and needn't reach their ends.
Inputs may be any that keep to these rules, and one draw needn't show every extreme that they name: `picks`: rows 4 * c to 4 * c + 3 are the query blocks held by index c of ctx, and blocks 4 * o to 4 * o + 3 are held by index o. Among the 8 entries of one such group of rows, at most 3 name blocks held by any one index of ctx; one index o, the same for every group, is named exactly 3 times by every group.
All inputs are finite; a program needn't handle non-finite values.
Results may differ from the reference program's by a relative error of at most 0.0039.
Values may be sent and summed in bfloat16 or wider, within the bound.
No kernel may reach another device: no remote copies, remote signals or barrier semaphores. Data moves between devices by JAX's collectives and lax.ppermute only.
A program may use at most 128 MiB of HBM per device.

```python
import jax
import jax.numpy as jnp
from jax import lax

HEADS = 16
HD = 128
BLOCK = 512
RSEL = 2
D = 2048
SEQ = 8192
NBLK = 16
LOCB = 4
CAP = 3


def draw_queries(key, part):
    base = jnp.clip(1.5 * jax.random.normal(jax.random.fold_in(key, 1), (SEQ, D)), -6.0, 6.0)
    return base.astype(jnp.bfloat16)


def draw_keys(key, part):
    base = jnp.clip(jax.random.normal(jax.random.fold_in(key, 2), (SEQ, D)), -6.0, 6.0)
    return base.astype(jnp.bfloat16)


def draw_picks(key, part):
    groups = NBLK // LOCB
    slots = LOCB * RSEL
    key_hot = jax.random.fold_in(key, 11)
    key_perm = jax.random.fold_in(key, 12)
    key_local = jax.random.fold_in(key, 13)
    hot = jax.random.randint(key_hot, (), 0, groups)
    entries = jnp.arange(groups * CAP, dtype=jnp.int32)
    owner_of = entries // CAP

    def one_group(group_key):
        rank = jax.random.permutation(jax.random.fold_in(group_key, 1), groups * CAP).astype(jnp.int32)
        score = jnp.where(owner_of == hot, entries - groups * CAP, rank)
        order = jnp.argsort(score, stable=True)
        chosen = owner_of[order][:slots]
        shuffle = jax.random.permutation(jax.random.fold_in(group_key, 2), slots)
        return chosen[shuffle]
    owners = jax.vmap(one_group)(jax.random.split(key_perm, groups))
    local = jax.random.randint(key_local, (groups, slots), 0, LOCB)
    return (owners * LOCB + local).reshape(NBLK, RSEL).astype(jnp.int32)


def block_levels(stream_key, dims, cuts, least, high):
    factor_of, own = 1.0, jax.random.fold_in(stream_key, 6)
    for position, shards_of in cuts:
        draws = jnp.exp(jax.random.uniform(jax.random.fold_in(own, position), (shards_of,), jnp.float32, least / len(cuts), high / len(cuts)))
        factor_of = factor_of * jnp.repeat(draws, dims[position] // shards_of).reshape([-1 if axis == position else 1 for axis in range(len(dims))])
    return factor_of


def normal_values(key, dims, width, reach, shards=(), kind=jnp.bfloat16):
    array = jax.random.normal(key, dims, jnp.float32) * width
    if len(shards) > 0:
        array = block_levels(key, dims, shards, -0.22, 0.18) * array
    return jnp.clip(array, min=-reach, max=reach).astype(kind)


def setup_inputs(seed: int = 0) -> dict:
    key_of = jax.random.split(jax.random.key(seed), 5)
    queries = draw_queries(jax.random.fold_in(key_of[4], 71), 0)
    keys = draw_keys(jax.random.fold_in(key_of[4], 71), 0)
    values = normal_values(key_of[2], (SEQ, D), 4.0, 24.0, ((0, 32),))
    picks = draw_picks(jax.random.fold_in(key_of[4], 71), 0)
    return {"queries": queries, "keys": keys, "values": values, "picks": picks}


def block_pair(query_block, key_block, value_block, score_scale):
    scores = jnp.einsum("qhd,khd->hqk", query_block.astype(jnp.float32), key_block.astype(jnp.float32)) * score_scale
    row_max = jnp.max(scores, axis=-1)
    exponent = jnp.exp(scores - row_max[..., None])
    row_sum = jnp.sum(exponent, axis=-1)
    weights = lax.optimization_barrier(exponent.astype(jnp.bfloat16))
    partial_out = jnp.einsum("hqk,khd->qhd", weights.astype(jnp.float32), value_block.astype(jnp.float32))
    return partial_out, row_max, row_sum


def reference(queries, keys, values, picks):
    score_scale = 1.0 / (HD ** 0.5)
    query_blocks = queries.reshape(NBLK, BLOCK, HEADS, HD)
    key_blocks = keys.reshape(NBLK, BLOCK, HEADS, HD)
    value_blocks = values.reshape(NBLK, BLOCK, HEADS, HD)

    def one_block(index):
        listed = lax.dynamic_index_in_dim(picks, index, 0, keepdims=False).astype(jnp.int32)
        block_ids = jnp.concatenate([index[None].astype(jnp.int32), listed])
        key_group = key_blocks[block_ids]
        value_group = value_blocks[block_ids]
        query_block = lax.dynamic_index_in_dim(query_blocks, index, 0, keepdims=False)

        def slot_pair(key_one, value_one):
            return block_pair(query_block, key_one, value_one, score_scale)

        outs_all, maxes_all, sums_all = jax.vmap(slot_pair)(key_group, value_group)
        overall = jnp.max(maxes_all, axis=0)
        factors = jnp.exp(maxes_all - overall[None])
        numer = jnp.sum(outs_all * jnp.transpose(factors, (0, 2, 1))[..., None], axis=0)
        denom = jnp.sum(sums_all * factors, axis=0)
        return (numer / jnp.transpose(denom, (1, 0))[..., None]).astype(jnp.bfloat16)

    result = lax.map(one_block, jnp.arange(NBLK, dtype=jnp.int32))
    return result.reshape(SEQ, HEADS * HD)
```

```python
import functools
import math

import jax
import jax.numpy as jnp
from jax import lax
from jax.experimental import pallas as pl
from jax.experimental.pallas import tpu as pltpu
from jax.sharding import PartitionSpec as P

HEADS = 16
HD = 128
BLOCK = 512
RSEL = 2
MAX_STEPS = 8
MIN_STEPS = 5
LATENCY = 2
ANY = pl.ANY


def plan_layout(local_blocks):
    send = 0
    pick = 2 * MAX_STEPS
    ready = pick + local_blocks * RSEL
    steps = ready + local_blocks
    return send, pick, ready, steps, steps + 1


def plan_kernel(groups, local_blocks, me_ref, picks_ref, out_ref):
    rows = max(8, 2 * groups)
    blocks = groups * local_blocks
    lanes = 128 * ((blocks + 127) // 128)
    send, pick, ready, steps, _ = plan_layout(local_blocks)
    f32 = jnp.float32
    lane_i = lax.broadcasted_iota(jnp.int32, (rows, lanes), 1)
    row_i = lax.broadcasted_iota(jnp.int32, (rows, lanes), 0)
    lane = lane_i.astype(f32)
    row = row_i.astype(f32)
    back = row >= groups
    place = jnp.where(back, row - groups, row)
    owner = jnp.zeros((rows, lanes), f32)
    for g in range(1, groups):
        owner = owner + jnp.where(lane_i >= g * local_blocks, 1.0, 0.0)
    origin = jnp.where(back, groups - 1 - owner, owner)
    far = jnp.full((rows, lanes), -1.0, f32)
    for entry in range(blocks * RSEL):
        query = entry // RSEL
        group = query // local_blocks
        named = picks_ref[query, entry % RSEL]
        target = jnp.where(back, f32(groups - 1 - group), f32(group))
        far = jnp.where(lane_i == named, jnp.maximum(far, target), far)
    never = f32(1e6)
    crosses = (far > place) & (origin <= place) & (row_i < 2 * groups)
    rank = (far * groups + (groups - 1 - origin)) * lanes + (lanes - 1 - lane)

    def step(t, carry):
        since, sent, came = carry
        now = t.astype(f32)
        able = crosses & (since <= now) & (sent < 0)
        key = jnp.where(able, rank, -1.0)
        best = jnp.max(key, axis=1, keepdims=True)
        goes = jnp.where(able & (key == best), 1.0, 0.0)
        sent = jnp.where(goes > 0, now, sent)
        lands = pltpu.roll(goes, 1, 0)
        came = jnp.where(lands > 0, now, came)
        since = jnp.where(lands > 0, now + LATENCY, since)
        return since, sent, came

    none = jnp.full((rows, lanes), -1.0, f32)
    held = place == origin
    since, sent, came = lax.fori_loop(0, MAX_STEPS, step, (jnp.where(held, 0.0, never), none, none))
    left = jnp.max(jnp.where(crosses & (sent < 0), 1.0, 0.0))
    last = jnp.max(sent)
    out_ref[steps] = jnp.where(left > 0, MAX_STEPS + 1, last.astype(jnp.int32) + 1)
    me = me_ref[0]
    for way in range(2):
        mine = row_i == (me if way == 0 else 2 * groups - 1 - me)
        source = jnp.where(held, lane - owner * local_blocks, came + local_blocks)
        for t in range(MAX_STEPS):
            code = jnp.sum(jnp.where(mine & (sent == t), source, 0.0))
            out_ref[send + 2 * t + way] = code.astype(jnp.int32)
    for block in range(local_blocks):
        late = jnp.int32(0)
        for slot in range(RSEL):
            named = picks_ref[me * local_blocks + block, slot]
            first = me * local_blocks
            below = named < first
            here = (named >= first) & (named < first + local_blocks)
            watched = jnp.where(below, me, 2 * groups - 1 - me)
            came_at = jnp.sum(jnp.where((row_i == watched) & (lane_i == named), came, 0.0)).astype(jnp.int32)
            code = jnp.where(here, named - first, came_at + local_blocks + jnp.where(below, 0, MAX_STEPS))
            out_ref[pick + block * RSEL + slot] = code
            late = jnp.maximum(late, jnp.where(here, 0, came_at + 1))
        out_ref[ready + block] = late


def make_plan(picks, groups, local_blocks):
    size = plan_layout(local_blocks)[-1]
    me = lax.axis_index("ctx").astype(jnp.int32).reshape(1)
    smem = pl.BlockSpec(memory_space=pltpu.SMEM)
    return pl.pallas_call(
        functools.partial(plan_kernel, groups, local_blocks),
        out_shape=jax.ShapeDtypeStruct((size,), jnp.int32),
        in_specs=[smem, smem],
        out_specs=smem,
        name="plan",
    )(me, picks)


def select_kernel(t, local_blocks, parts, count, table_ref, own_ref, *refs):
    came = (refs[:count], refs[count : 2 * count])
    outs = refs[2 * count : 2 * count + 2]
    buf, sems = refs[2 * count + 2 :]
    for way in range(2):
        code = table_ref[2 * t + way]

        @pl.when(code < local_blocks)
        def _():
            pltpu.make_async_copy(own_ref.at[pl.ds(code * parts, parts)], buf.at[way], sems.at[way]).start()

        for slot in range(count):

            @pl.when(code == local_blocks + slot)
            def _():
                pltpu.make_async_copy(came[way][slot], buf.at[way], sems.at[way]).start()

    for way in range(2):
        pltpu.make_async_copy(own_ref.at[pl.ds(0, parts)], buf.at[way], sems.at[way]).wait()
        pltpu.make_async_copy(buf.at[way], outs[way], sems.at[way]).start()
    for way in range(2):
        pltpu.make_async_copy(buf.at[way], outs[way], sems.at[way]).wait()


def select(t, local_blocks, parts, table, own, came_up, came_down):
    count = len(came_up)
    any_spec = pl.BlockSpec(memory_space=ANY)
    shape = jax.ShapeDtypeStruct((parts,) + own.shape[1:], own.dtype)
    return pl.pallas_call(
        functools.partial(select_kernel, t, local_blocks, parts, count),
        out_shape=(shape, shape),
        in_specs=[pl.BlockSpec(memory_space=pltpu.SMEM)] + [any_spec] * (1 + 2 * count),
        out_specs=(any_spec, any_spec),
        scratch_shapes=[pltpu.VMEM((2,) + shape.shape, shape.dtype), pltpu.SemaphoreType.DMA((2,))],
        cost_estimate=pl.CostEstimate(flops=0, bytes_accessed=4 << 20, transcendentals=0),
        name="select",
    )(table, own, *came_up, *came_down)


def attend_kernel(low, high, local_blocks, parts, count, chained, table_ref, q_ref, own_ref, *refs):
    came = (refs[:count], refs[count : 2 * count])
    refs = refs[2 * count + (1 if chained else 0) :]
    out_ref, q_buf, kv_buf, o_buf, in_sems, out_sems = refs
    _, pick, ready, _, _ = plan_layout(local_blocks)
    rows = q_ref.shape[1]
    width = q_ref.shape[2]
    heads_here = width // HD
    scale = math.log2(math.e) / math.sqrt(HD)
    slots = RSEL + 1

    def due(block):
        late = table_ref[ready + block]
        return (late > low) & (late <= high) if low >= 0 else late <= high

    def own_part(block):
        return own_ref.at[pl.ds(block * parts, parts)]

    for block in range(local_blocks):

        @pl.when(due(block))
        def _():
            pltpu.make_async_copy(q_ref.at[pl.ds(block * parts, parts)], q_buf.at[block], in_sems.at[block, slots]).start()
            pltpu.make_async_copy(own_part(block), kv_buf.at[block, 0], in_sems.at[block, 0]).start()
            for slot in range(RSEL):
                code = table_ref[pick + block * RSEL + slot]
                target = kv_buf.at[block, 1 + slot]
                sem = in_sems.at[block, 1 + slot]

                @pl.when(code < local_blocks)
                def _():
                    pltpu.make_async_copy(own_part(code), target, sem).start()

                for way in range(2):
                    for step in range(count):

                        @pl.when(code == local_blocks + way * MAX_STEPS + step)
                        def _():
                            pltpu.make_async_copy(came[way][step], target, sem).start()

    def one(block, _):
        @pl.when(due(block))
        def _():
            pltpu.make_async_copy(q_ref.at[pl.ds(0, parts)], q_buf.at[block], in_sems.at[block, slots]).wait()
            for slot in range(slots):
                pltpu.make_async_copy(own_part(0), kv_buf.at[block, slot], in_sems.at[block, slot]).wait()
            for part in range(parts):
                for head in range(heads_here):
                    cols = slice(head * HD, (head + 1) * HD)
                    q = q_buf[block, part, :, cols]
                    scores = []
                    for slot in range(slots):
                        for half in range(parts):
                            k = kv_buf[block, slot, half, 0, :, cols]
                            scores.append(
                                lax.dot_general(q, k, (((1,), (1,)), ((), ())), preferred_element_type=jnp.float32)
                            )
                    top = functools.reduce(jnp.maximum, [jnp.max(s, axis=1, keepdims=True) for s in scores])
                    total = jnp.zeros((rows, HD), jnp.float32)
                    mass = jnp.zeros((rows, 1), jnp.float32)
                    index = 0
                    for slot in range(slots):
                        for half in range(parts):
                            v = kv_buf[block, slot, half, 1, :, cols]
                            w = jnp.exp2((scores[index] - top) * scale)
                            mass = mass + jnp.sum(w, axis=1, keepdims=True)
                            total = total + jnp.dot(w.astype(jnp.bfloat16), v, preferred_element_type=jnp.float32)
                            index += 1
                    o_buf[block, part, :, cols] = (total / mass).astype(jnp.bfloat16)
            pltpu.make_async_copy(o_buf.at[block], out_ref.at[pl.ds(block * parts, parts)], out_sems.at[block]).start()

        return 0

    lax.fori_loop(0, local_blocks, one, 0)
    for block in range(local_blocks):

        @pl.when(due(block))
        def _():
            pltpu.make_async_copy(o_buf.at[block], out_ref.at[pl.ds(block * parts, parts)], out_sems.at[block]).wait()


def attend(low, high, local_blocks, parts, table, q, own, came_up, came_down, so_far):
    count = len(came_up)
    any_spec = pl.BlockSpec(memory_space=ANY)
    chained = so_far is not None
    kv_shape = own.shape[1:]
    inputs = [table, q, own, *came_up, *came_down] + ([so_far] if chained else [])
    return pl.pallas_call(
        functools.partial(attend_kernel, low, high, local_blocks, parts, count, chained),
        out_shape=jax.ShapeDtypeStruct(q.shape, q.dtype),
        in_specs=[pl.BlockSpec(memory_space=pltpu.SMEM)] + [any_spec] * (len(inputs) - 1),
        out_specs=any_spec,
        scratch_shapes=[
            pltpu.VMEM((local_blocks, parts) + q.shape[1:], q.dtype),
            pltpu.VMEM((local_blocks, RSEL + 1, parts) + kv_shape, q.dtype),
            pltpu.VMEM((local_blocks, parts) + q.shape[1:], q.dtype),
            pltpu.SemaphoreType.DMA((local_blocks, RSEL + 2)),
            pltpu.SemaphoreType.DMA((local_blocks,)),
        ],
        input_output_aliases={len(inputs) - 1: 0} if chained else {},
        compiler_params=pltpu.CompilerParams(vmem_limit_bytes=40 << 20),
        cost_estimate=pl.CostEstimate(flops=1 << 30, bytes_accessed=8 << 20, transcendentals=1 << 21),
        name="attend",
    )(*inputs)


def shift(x, by, groups):
    pairs = [(i, i + by) for i in range(groups) if 0 <= i + by < groups]
    return lax.ppermute(x, "ctx", pairs)


def by_head(x, head_count):
    rows, width = x.shape
    return x.reshape(rows, head_count, width // head_count).transpose(1, 0, 2)


def swap(x):
    return lax.all_to_all(x, "head", split_axis=0, concat_axis=0, tiled=True)


def hops(steps, groups, local_blocks, parts, q_mine, own, table):
    came_up, came_down = [], []
    for t in range(steps):
        known = max(0, t + 1 - LATENCY)
        up, down = select(t, local_blocks, parts, table, own, came_up[:known], came_down[:known])
        came_up.append(shift(up, 1, groups))
        came_down.append(shift(down, -1, groups))
    q = swap(q_mine)
    out, low = None, -1
    for high in (steps - 3, steps - 1, steps):
        out = attend(low, high, local_blocks, parts, table, q, own, came_up[:high], came_down[:high], out)
        low = high
    return swap(out)


def local(queries, keys, values, picks):
    head_count = lax.axis_size("head")
    groups = lax.axis_size("ctx")
    tok_rows, model = queries.shape
    local_blocks = tok_rows * head_count // BLOCK
    parts = BLOCK // tok_rows
    q_mine = by_head(queries, head_count)
    kv_mine = jnp.stack([by_head(keys, head_count), by_head(values, head_count)], axis=1)
    own = swap(kv_mine)
    if groups * local_blocks > 16:
        out = by_queries(q_mine, own, picks, groups, local_blocks)
    else:
        table = make_plan(picks, groups, local_blocks)
        branches = [
            functools.partial(hops, n, groups, local_blocks, parts) for n in range(MIN_STEPS, MAX_STEPS + 1)
        ]
        branches.append(lambda q, kv, tab: by_queries(q, kv, picks, groups, local_blocks))
        steps = table[plan_layout(local_blocks)[3]]
        which = jnp.clip(steps - MIN_STEPS, 0, len(branches) - 1)
        out = lax.switch(which, branches, q_mine, own, table)
    return out.transpose(1, 0, 2).reshape(tok_rows, model)


def block_pair(query_block, key_block, value_block):
    scores = jnp.einsum("qhd,khd->hqk", query_block, key_block, preferred_element_type=jnp.float32)
    scores = scores * (1.0 / math.sqrt(HD))
    row_max = jnp.max(scores, axis=-1)
    exponent = jnp.exp(scores - row_max[..., None])
    row_sum = jnp.sum(exponent, axis=-1)
    partial_out = jnp.einsum(
        "hqk,khd->qhd", exponent.astype(jnp.bfloat16), value_block, preferred_element_type=jnp.float32
    )
    return partial_out, row_max, row_sum


def route_tables(picks, local_blocks, ctx_count):
    slots = local_blocks * RSEL
    owners = (picks // local_blocks).reshape(ctx_count, slots)
    within = (picks % local_blocks).reshape(ctx_count, slots)
    owner_ids = jnp.arange(ctx_count, dtype=jnp.int32)
    one_hot = (owners[:, :, None] == owner_ids[None, None, :]).astype(jnp.int32)
    running = jnp.cumsum(one_hot, axis=1)
    position = jnp.sum(one_hot * running, axis=-1) - 1
    return owners, within, position


def by_queries(q_mine, own, picks, ctx_count, local_blocks):
    head_count, tok_rows, width = q_mine.shape
    heads_here = width // HD
    my_index = lax.axis_index("ctx")
    shape = (local_blocks, BLOCK, heads_here, HD)
    q_blocks = swap(q_mine).reshape(shape)
    k_blocks = own[:, 0].reshape(shape)
    v_blocks = own[:, 1].reshape(shape)
    capacity = (local_blocks * RSEL + ctx_count - 1) // ctx_count + 1
    slots = local_blocks * RSEL
    owners, within, position = route_tables(picks, local_blocks, ctx_count)
    mine_owner = lax.dynamic_index_in_dim(owners, my_index, 0, keepdims=False)
    mine_pos = lax.dynamic_index_in_dim(position, my_index, 0, keepdims=False)
    slot_ids = jnp.arange(capacity, dtype=jnp.int32)
    asked = (owners == my_index)[:, :, None] & (position[:, :, None] == slot_ids[None, None, :])
    wanted = jnp.sum(asked.astype(jnp.int32) * within[:, :, None], axis=1)
    pick_back = mine_owner * capacity + mine_pos
    own_out, own_max, own_sum = lax.map(lambda b: block_pair(*b), (q_blocks, k_blocks, v_blocks))
    owner_ids = jnp.arange(ctx_count, dtype=jnp.int32)
    chosen = (mine_owner[:, None, None] == owner_ids[None, :, None]) & (
        mine_pos[:, None, None] == slot_ids[None, None, :]
    )
    query_of_slot = jnp.arange(slots, dtype=jnp.int32) // RSEL
    source_block = jnp.sum(chosen.astype(jnp.int32) * query_of_slot[:, None, None], axis=0)
    arrived = lax.all_to_all(q_blocks[source_block], "ctx", split_axis=0, concat_axis=0, tiled=True)

    def owner_pair(items):
        query_block, block_index = items
        return block_pair(query_block, k_blocks[block_index], v_blocks[block_index])

    far = lax.map(owner_pair, (arrived.reshape((-1,) + shape[1:]), wanted.reshape(-1)))
    back = [
        lax.all_to_all(x.reshape((ctx_count, capacity) + x.shape[1:]), "ctx", split_axis=0, concat_axis=0, tiled=True)
        for x in far
    ]
    back = [x.reshape((-1,) + x.shape[2:])[pick_back] for x in back]
    far_out, far_max, far_sum = [x.reshape((local_blocks, RSEL) + x.shape[1:]) for x in back]
    overall = jnp.maximum(own_max, jnp.max(far_max, axis=1))
    own_factor = jnp.exp(own_max - overall)
    far_factor = jnp.exp(far_max - overall[:, None])
    numer = own_out * jnp.transpose(own_factor, (0, 2, 1))[..., None]
    numer = numer + jnp.sum(far_out * jnp.transpose(far_factor, (0, 1, 3, 2))[..., None], axis=1)
    denom = own_sum * own_factor + jnp.sum(far_sum * far_factor, axis=1)
    result = (numer / jnp.transpose(denom, (0, 2, 1))[..., None]).astype(jnp.bfloat16)
    return swap(result.reshape(head_count, tok_rows, width))


def solution(mesh):
    placed = (P(("ctx", "head"), None), P(("ctx", "head"), None), P(("ctx", "head"), None), P())
    return jax.shard_map(
        local, mesh=mesh, in_specs=placed, out_specs=P(("ctx", "head"), None), check_vma=False
    )
```

```python
import functools
import math

import jax
import jax.numpy as jnp
from jax import lax
from jax.experimental import pallas as pl
from jax.experimental.pallas import tpu as pltpu
from jax.sharding import PartitionSpec as P

HEADS = 16
HD = 128
BLOCK = 512
RSEL = 2
MAX_STEPS = 8
MIN_STEPS = 5
LATENCY = 2
ANY = pl.ANY


def plan_layout(local_blocks):
    send = 0
    pick = 2 * MAX_STEPS
    ready = pick + local_blocks * RSEL
    steps = ready + local_blocks
    return send, pick, ready, steps, steps + 1


def plan_kernel(groups, local_blocks, me_ref, picks_ref, out_ref):
    rows = max(8, 2 * groups)
    blocks = groups * local_blocks
    lanes = 128 * ((blocks + 127) // 128)
    send, pick, ready, steps, _ = plan_layout(local_blocks)
    f32 = jnp.float32
    lane_i = lax.broadcasted_iota(jnp.int32, (rows, lanes), 1)
    row_i = lax.broadcasted_iota(jnp.int32, (rows, lanes), 0)
    lane = lane_i.astype(f32)
    row = row_i.astype(f32)
    back = row >= groups
    place = jnp.where(back, row - groups, row)
    owner = jnp.zeros((rows, lanes), f32)
    for g in range(1, groups):
        owner = owner + jnp.where(lane_i >= g * local_blocks, 1.0, 0.0)
    origin = jnp.where(back, groups - 1 - owner, owner)
    far = jnp.full((rows, lanes), -1.0, f32)
    for entry in range(blocks * RSEL):
        query = entry // RSEL
        group = query // local_blocks
        named = picks_ref[query, entry % RSEL]
        target = jnp.where(back, f32(groups - 1 - group), f32(group))
        far = jnp.where(lane_i == named, jnp.maximum(far, target), far)
    never = f32(1e6)
    crosses = (far > place) & (origin <= place) & (row_i < 2 * groups)
    rank = (far * groups + (groups - 1 - origin)) * lanes + (lanes - 1 - lane)

    def step(t, carry):
        since, sent, came = carry
        now = t.astype(f32)
        able = crosses & (since <= now) & (sent < 0)
        key = jnp.where(able, rank, -1.0)
        best = jnp.max(key, axis=1, keepdims=True)
        goes = jnp.where(able & (key == best), 1.0, 0.0)
        sent = jnp.where(goes > 0, now, sent)
        lands = pltpu.roll(goes, 1, 0)
        came = jnp.where(lands > 0, now, came)
        since = jnp.where(lands > 0, now + LATENCY, since)
        return since, sent, came

    none = jnp.full((rows, lanes), -1.0, f32)
    held = place == origin
    since, sent, came = lax.fori_loop(0, MAX_STEPS, step, (jnp.where(held, 0.0, never), none, none))
    left = jnp.max(jnp.where(crosses & (sent < 0), 1.0, 0.0))
    last = jnp.max(sent)
    out_ref[steps] = jnp.where(left > 0, MAX_STEPS + 1, last.astype(jnp.int32) + 1)
    me = me_ref[0]
    for way in range(2):
        mine = row_i == (me if way == 0 else 2 * groups - 1 - me)
        source = jnp.where(held, lane - owner * local_blocks, came + local_blocks)
        for t in range(MAX_STEPS):
            code = jnp.sum(jnp.where(mine & (sent == t), source, 0.0))
            out_ref[send + 2 * t + way] = code.astype(jnp.int32)
    for block in range(local_blocks):
        late = jnp.int32(0)
        for slot in range(RSEL):
            named = picks_ref[me * local_blocks + block, slot]
            first = me * local_blocks
            below = named < first
            here = (named >= first) & (named < first + local_blocks)
            watched = jnp.where(below, me, 2 * groups - 1 - me)
            came_at = jnp.sum(jnp.where((row_i == watched) & (lane_i == named), came, 0.0)).astype(jnp.int32)
            code = jnp.where(here, named - first, came_at + local_blocks + jnp.where(below, 0, MAX_STEPS))
            out_ref[pick + block * RSEL + slot] = code
            late = jnp.maximum(late, jnp.where(here, 0, came_at + 1))
        out_ref[ready + block] = late


def make_plan(picks, groups, local_blocks):
    size = plan_layout(local_blocks)[-1]
    me = lax.axis_index("ctx").astype(jnp.int32).reshape(1)
    smem = pl.BlockSpec(memory_space=pltpu.SMEM)
    return pl.pallas_call(
        functools.partial(plan_kernel, groups, local_blocks),
        out_shape=jax.ShapeDtypeStruct((size,), jnp.int32),
        in_specs=[smem, smem],
        out_specs=smem,
        name="plan",
    )(me, picks)


def select_kernel(t, local_blocks, parts, count, table_ref, own_ref, *refs):
    came = (refs[:count], refs[count : 2 * count])
    outs = refs[2 * count : 2 * count + 2]
    buf, sems = refs[2 * count + 2 :]
    for way in range(2):
        code = table_ref[2 * t + way]

        @pl.when(code < local_blocks)
        def _():
            pltpu.make_async_copy(own_ref.at[pl.ds(code * parts, parts)], buf.at[way], sems.at[way]).start()

        for slot in range(count):

            @pl.when(code == local_blocks + slot)
            def _():
                pltpu.make_async_copy(came[way][slot], buf.at[way], sems.at[way]).start()

    for way in range(2):
        pltpu.make_async_copy(own_ref.at[pl.ds(0, parts)], buf.at[way], sems.at[way]).wait()
        pltpu.make_async_copy(buf.at[way], outs[way], sems.at[way]).start()
    for way in range(2):
        pltpu.make_async_copy(buf.at[way], outs[way], sems.at[way]).wait()


def select(t, local_blocks, parts, table, own, came_up, came_down):
    count = len(came_up)
    any_spec = pl.BlockSpec(memory_space=ANY)
    shape = jax.ShapeDtypeStruct((parts,) + own.shape[1:], own.dtype)
    return pl.pallas_call(
        functools.partial(select_kernel, t, local_blocks, parts, count),
        out_shape=(shape, shape),
        in_specs=[pl.BlockSpec(memory_space=pltpu.SMEM)] + [any_spec] * (1 + 2 * count),
        out_specs=(any_spec, any_spec),
        scratch_shapes=[pltpu.VMEM((2,) + shape.shape, shape.dtype), pltpu.SemaphoreType.DMA((2,))],
        compiler_params=pltpu.CompilerParams(vmem_limit_bytes=4 << 20),
        cost_estimate=pl.CostEstimate(flops=0, bytes_accessed=4 << 20, transcendentals=0),
        name="select",
    )(table, own, *came_up, *came_down)


def attend_kernel(low, high, local_blocks, parts, count, chained, table_ref, q_ref, own_ref, *refs):
    came = (refs[:count], refs[count : 2 * count])
    refs = refs[2 * count + (1 if chained else 0) :]
    out_ref, q_buf, kv_buf, o_buf, in_sems, out_sems = refs
    _, pick, ready, _, _ = plan_layout(local_blocks)
    rows = q_ref.shape[1]
    width = q_ref.shape[2]
    heads_here = width // HD
    scale = math.log2(math.e) / math.sqrt(HD)
    slots = RSEL + 1

    def due(block):
        late = table_ref[ready + block]
        return (late > low) & (late <= high) if low >= 0 else late <= high

    def own_part(block):
        return own_ref.at[pl.ds(block * parts, parts)]

    def fetch(block, _):
        @pl.when(due(block))
        def _():
            pltpu.make_async_copy(q_ref.at[pl.ds(block * parts, parts)], q_buf.at[block], in_sems.at[block, slots]).start()
            pltpu.make_async_copy(own_part(block), kv_buf.at[block, 0], in_sems.at[block, 0]).start()
            for slot in range(RSEL):
                code = table_ref[pick + block * RSEL + slot]
                target = kv_buf.at[block, 1 + slot]
                sem = in_sems.at[block, 1 + slot]

                @pl.when(code < local_blocks)
                def _():
                    pltpu.make_async_copy(own_part(code), target, sem).start()

                for way in range(2):
                    for step in range(count):

                        @pl.when(code == local_blocks + way * MAX_STEPS + step)
                        def _():
                            pltpu.make_async_copy(came[way][step], target, sem).start()

        return 0

    def tile(block, part, head):
        cols = pl.ds(pl.multiple_of(head * HD, HD), HD)
        q = q_buf[block, part, :, cols]
        scores = []
        for slot in range(slots):
            for half in range(parts):
                k = kv_buf[block, slot, half, 0, :, cols]
                scores.append(lax.dot_general(q, k, (((1,), (1,)), ((), ())), preferred_element_type=jnp.float32))
        top = functools.reduce(jnp.maximum, [jnp.max(s, axis=1, keepdims=True) for s in scores])
        total = jnp.zeros((rows, HD), jnp.float32)
        mass = jnp.zeros((rows, 1), jnp.float32)
        for index, s in enumerate(scores):
            v = kv_buf[block, index // parts, index % parts, 1, :, cols]
            w = jnp.exp2((s - top) * scale)
            mass = mass + jnp.sum(w, axis=1, keepdims=True)
            total = total + jnp.dot(w.astype(jnp.bfloat16), v, preferred_element_type=jnp.float32)
        o_buf[block, part, :, cols] = (total / mass).astype(jnp.bfloat16)

    def one(block, _):
        @pl.when(due(block))
        def _():
            pltpu.make_async_copy(q_ref.at[pl.ds(0, parts)], q_buf.at[block], in_sems.at[block, slots]).wait()
            for slot in range(slots):
                pltpu.make_async_copy(own_part(0), kv_buf.at[block, slot], in_sems.at[block, slot]).wait()

            def at(i, _):
                tile(block, i // heads_here, i % heads_here)
                return 0

            lax.fori_loop(0, parts * heads_here, at, 0)
            pltpu.make_async_copy(o_buf.at[block], out_ref.at[pl.ds(block * parts, parts)], out_sems.at[block]).start()

        return 0

    def flush(block, _):
        @pl.when(due(block))
        def _():
            pltpu.make_async_copy(o_buf.at[block], out_ref.at[pl.ds(block * parts, parts)], out_sems.at[block]).wait()

        return 0

    lax.fori_loop(0, local_blocks, fetch, 0)
    lax.fori_loop(0, local_blocks, one, 0)
    lax.fori_loop(0, local_blocks, flush, 0)


def attend(low, high, local_blocks, parts, table, q, own, came_up, came_down, so_far):
    count = len(came_up)
    any_spec = pl.BlockSpec(memory_space=ANY)
    chained = so_far is not None
    kv_shape = own.shape[1:]
    inputs = [table, q, own, *came_up, *came_down] + ([so_far] if chained else [])
    return pl.pallas_call(
        functools.partial(attend_kernel, low, high, local_blocks, parts, count, chained),
        out_shape=jax.ShapeDtypeStruct(q.shape, q.dtype),
        in_specs=[pl.BlockSpec(memory_space=pltpu.SMEM)] + [any_spec] * (len(inputs) - 1),
        out_specs=any_spec,
        scratch_shapes=[
            pltpu.VMEM((local_blocks, parts) + q.shape[1:], q.dtype),
            pltpu.VMEM((local_blocks, RSEL + 1, parts) + kv_shape, q.dtype),
            pltpu.VMEM((local_blocks, parts) + q.shape[1:], q.dtype),
            pltpu.SemaphoreType.DMA((local_blocks, RSEL + 2)),
            pltpu.SemaphoreType.DMA((local_blocks,)),
        ],
        input_output_aliases={len(inputs) - 1: 0} if chained else {},
        compiler_params=pltpu.CompilerParams(vmem_limit_bytes=18 << 20),
        cost_estimate=pl.CostEstimate(flops=1 << 30, bytes_accessed=8 << 20, transcendentals=1 << 21),
        name="attend",
    )(*inputs)


def shift(x, by, groups):
    pairs = [(i, i + by) for i in range(groups) if 0 <= i + by < groups]
    return lax.ppermute(x, "ctx", pairs)


def pack_kernel(head_count, *refs):
    ins, out = refs[:-1], refs[-1]
    cols = out.shape[-1]
    for i, ref in enumerate(ins):
        for g in range(head_count):
            out[g, i] = ref[:, g * cols : (g + 1) * cols]


def pack(head_count, *arrays):
    rows, width = arrays[0].shape
    cols = width // head_count
    pieces = 4
    some = rows // pieces
    return pl.pallas_call(
        functools.partial(pack_kernel, head_count),
        grid=(pieces,),
        out_shape=jax.ShapeDtypeStruct((head_count, len(arrays), rows, cols), arrays[0].dtype),
        in_specs=[pl.BlockSpec((some, width), lambda r: (r, 0))] * len(arrays),
        out_specs=pl.BlockSpec((head_count, len(arrays), some, cols), lambda r: (0, 0, r, 0)),
        name="pack",
    )(*arrays)


def swap(x):
    return lax.all_to_all(x, "head", split_axis=0, concat_axis=0, tiled=True)


def hops(steps, groups, local_blocks, parts, q_mine, own, table):
    came_up, came_down = [], []
    for t in range(steps):
        known = max(0, t + 1 - LATENCY)
        up, down = select(t, local_blocks, parts, table, own, came_up[:known], came_down[:known])
        came_up.append(shift(up, 1, groups))
        came_down.append(shift(down, -1, groups))
    q = swap(q_mine)
    out, low = None, -1
    for high in (steps - 3, steps - 1, steps):
        out = attend(low, high, local_blocks, parts, table, q, own, came_up[:high], came_down[:high], out)
        low = high
    return swap(out)


def local(queries, keys, values, picks):
    head_count = lax.axis_size("head")
    groups = lax.axis_size("ctx")
    tok_rows, model = queries.shape
    local_blocks = tok_rows * head_count // BLOCK
    parts = BLOCK // tok_rows
    own = swap(pack(head_count, keys, values))
    q_mine = pack(head_count, queries)[:, 0]
    if groups * local_blocks > 16:
        out = by_queries(q_mine, own, picks, groups, local_blocks)
    else:
        table = make_plan(picks, groups, local_blocks)
        branches = [
            functools.partial(hops, n, groups, local_blocks, parts) for n in range(MIN_STEPS, MAX_STEPS + 1)
        ]
        branches.append(lambda q, kv, tab: by_queries(q, kv, picks, groups, local_blocks))
        steps = table[plan_layout(local_blocks)[3]]
        which = jnp.clip(steps - MIN_STEPS, 0, len(branches) - 1)
        out = lax.switch(which, branches, q_mine, own, table)
    return out.transpose(1, 0, 2).reshape(tok_rows, model)


def block_pair(query_block, key_block, value_block):
    scores = jnp.einsum("qhd,khd->hqk", query_block, key_block, preferred_element_type=jnp.float32)
    scores = scores * (1.0 / math.sqrt(HD))
    row_max = jnp.max(scores, axis=-1)
    exponent = jnp.exp(scores - row_max[..., None])
    row_sum = jnp.sum(exponent, axis=-1)
    partial_out = jnp.einsum(
        "hqk,khd->qhd", exponent.astype(jnp.bfloat16), value_block, preferred_element_type=jnp.float32
    )
    return partial_out, row_max, row_sum


def route_tables(picks, local_blocks, ctx_count):
    slots = local_blocks * RSEL
    owners = (picks // local_blocks).reshape(ctx_count, slots)
    within = (picks % local_blocks).reshape(ctx_count, slots)
    owner_ids = jnp.arange(ctx_count, dtype=jnp.int32)
    one_hot = (owners[:, :, None] == owner_ids[None, None, :]).astype(jnp.int32)
    running = jnp.cumsum(one_hot, axis=1)
    position = jnp.sum(one_hot * running, axis=-1) - 1
    return owners, within, position


def by_queries(q_mine, own, picks, ctx_count, local_blocks):
    head_count, tok_rows, width = q_mine.shape
    heads_here = width // HD
    my_index = lax.axis_index("ctx")
    shape = (local_blocks, BLOCK, heads_here, HD)
    q_blocks = swap(q_mine).reshape(shape)
    k_blocks = own[:, 0].reshape(shape)
    v_blocks = own[:, 1].reshape(shape)
    capacity = (local_blocks * RSEL + ctx_count - 1) // ctx_count + 1
    slots = local_blocks * RSEL
    owners, within, position = route_tables(picks, local_blocks, ctx_count)
    mine_owner = lax.dynamic_index_in_dim(owners, my_index, 0, keepdims=False)
    mine_pos = lax.dynamic_index_in_dim(position, my_index, 0, keepdims=False)
    slot_ids = jnp.arange(capacity, dtype=jnp.int32)
    asked = (owners == my_index)[:, :, None] & (position[:, :, None] == slot_ids[None, None, :])
    wanted = jnp.sum(asked.astype(jnp.int32) * within[:, :, None], axis=1)
    pick_back = mine_owner * capacity + mine_pos
    own_out, own_max, own_sum = lax.map(lambda b: block_pair(*b), (q_blocks, k_blocks, v_blocks))
    owner_ids = jnp.arange(ctx_count, dtype=jnp.int32)
    chosen = (mine_owner[:, None, None] == owner_ids[None, :, None]) & (
        mine_pos[:, None, None] == slot_ids[None, None, :]
    )
    query_of_slot = jnp.arange(slots, dtype=jnp.int32) // RSEL
    source_block = jnp.sum(chosen.astype(jnp.int32) * query_of_slot[:, None, None], axis=0)
    arrived = lax.all_to_all(q_blocks[source_block], "ctx", split_axis=0, concat_axis=0, tiled=True)

    def owner_pair(items):
        query_block, block_index = items
        return block_pair(query_block, k_blocks[block_index], v_blocks[block_index])

    far = lax.map(owner_pair, (arrived.reshape((-1,) + shape[1:]), wanted.reshape(-1)))
    back = [
        lax.all_to_all(x.reshape((ctx_count, capacity) + x.shape[1:]), "ctx", split_axis=0, concat_axis=0, tiled=True)
        for x in far
    ]
    back = [x.reshape((-1,) + x.shape[2:])[pick_back] for x in back]
    far_out, far_max, far_sum = [x.reshape((local_blocks, RSEL) + x.shape[1:]) for x in back]
    overall = jnp.maximum(own_max, jnp.max(far_max, axis=1))
    own_factor = jnp.exp(own_max - overall)
    far_factor = jnp.exp(far_max - overall[:, None])
    numer = own_out * jnp.transpose(own_factor, (0, 2, 1))[..., None]
    numer = numer + jnp.sum(far_out * jnp.transpose(far_factor, (0, 1, 3, 2))[..., None], axis=1)
    denom = own_sum * own_factor + jnp.sum(far_sum * far_factor, axis=1)
    result = (numer / jnp.transpose(denom, (0, 2, 1))[..., None]).astype(jnp.bfloat16)
    return swap(result.reshape(head_count, tok_rows, width))


def solution(mesh):
    placed = (P(("ctx", "head"), None), P(("ctx", "head"), None), P(("ctx", "head"), None), P())
    return jax.shard_map(
        local, mesh=mesh, in_specs=placed, out_specs=P(("ctx", "head"), None), check_vma=False
    )
```

```python
import functools
import math

import jax
import jax.numpy as jnp
from jax import lax
from jax.experimental import pallas as pl
from jax.experimental.pallas import tpu as pltpu
from jax.sharding import PartitionSpec as P

HEADS = 16
HD = 128
BLOCK = 512
RSEL = 2
MAX_STEPS = 8
MIN_STEPS = 6
LATENCY = 2
ANY = pl.ANY


def plan_layout(local_blocks):
    send = 0
    pick = 2 * MAX_STEPS
    ready = pick + local_blocks * RSEL
    steps = ready + local_blocks
    return send, pick, ready, steps, steps + 1


def plan_kernel(groups, local_blocks, me_ref, picks_ref, out_ref):
    rows = max(8, 2 * groups)
    blocks = groups * local_blocks
    lanes = 128 * ((blocks + 127) // 128)
    send, pick, ready, steps, _ = plan_layout(local_blocks)
    f32 = jnp.float32
    lane_i = lax.broadcasted_iota(jnp.int32, (rows, lanes), 1)
    row_i = lax.broadcasted_iota(jnp.int32, (rows, lanes), 0)
    lane = lane_i.astype(f32)
    row = row_i.astype(f32)
    back = row >= groups
    place = jnp.where(back, row - groups, row)
    owner = jnp.zeros((rows, lanes), f32)
    for g in range(1, groups):
        owner = owner + jnp.where(lane_i >= g * local_blocks, 1.0, 0.0)
    origin = jnp.where(back, groups - 1 - owner, owner)
    far = jnp.full((rows, lanes), -1.0, f32)
    for entry in range(blocks * RSEL):
        query = entry // RSEL
        group = query // local_blocks
        named = picks_ref[query, entry % RSEL]
        target = jnp.where(back, f32(groups - 1 - group), f32(group))
        far = jnp.where(lane_i == named, jnp.maximum(far, target), far)
    never = f32(1e6)
    crosses = (far > place) & (origin <= place) & (row_i < 2 * groups)
    rank = (far * groups + (groups - 1 - origin)) * lanes + (lanes - 1 - lane)

    def step(t, carry):
        since, sent, came = carry
        now = t.astype(f32)
        able = crosses & (since <= now) & (sent < 0)
        key = jnp.where(able, rank, -1.0)
        best = jnp.max(key, axis=1, keepdims=True)
        goes = jnp.where(able & (key == best), 1.0, 0.0)
        sent = jnp.where(goes > 0, now, sent)
        lands = pltpu.roll(goes, 1, 0)
        came = jnp.where(lands > 0, now, came)
        since = jnp.where(lands > 0, now + LATENCY, since)
        return since, sent, came

    none = jnp.full((rows, lanes), -1.0, f32)
    held = place == origin
    since, sent, came = lax.fori_loop(0, MAX_STEPS, step, (jnp.where(held, 0.0, never), none, none))
    left = jnp.max(jnp.where(crosses & (sent < 0), 1.0, 0.0))
    last = jnp.max(sent)
    out_ref[steps] = jnp.where(left > 0, MAX_STEPS + 1, last.astype(jnp.int32) + 1)
    me = me_ref[0]
    for way in range(2):
        mine = row_i == (me if way == 0 else 2 * groups - 1 - me)
        source = jnp.where(held, lane - owner * local_blocks, came + local_blocks)
        for t in range(MAX_STEPS):
            code = jnp.sum(jnp.where(mine & (sent == t), source, 0.0))
            out_ref[send + 2 * t + way] = code.astype(jnp.int32)
    for block in range(local_blocks):
        late = jnp.int32(0)
        for slot in range(RSEL):
            named = picks_ref[me * local_blocks + block, slot]
            first = me * local_blocks
            below = named < first
            here = (named >= first) & (named < first + local_blocks)
            watched = jnp.where(below, me, 2 * groups - 1 - me)
            came_at = jnp.sum(jnp.where((row_i == watched) & (lane_i == named), came, 0.0)).astype(jnp.int32)
            code = jnp.where(here, named - first, came_at + local_blocks + jnp.where(below, 0, MAX_STEPS))
            out_ref[pick + block * RSEL + slot] = code
            late = jnp.maximum(late, jnp.where(here, 0, came_at + 1))
        out_ref[ready + block] = late


def make_plan(picks, groups, local_blocks):
    size = plan_layout(local_blocks)[-1]
    me = lax.axis_index("ctx").astype(jnp.int32).reshape(1)
    smem = pl.BlockSpec(memory_space=pltpu.SMEM)
    return pl.pallas_call(
        functools.partial(plan_kernel, groups, local_blocks),
        out_shape=jax.ShapeDtypeStruct((size,), jnp.int32),
        in_specs=[smem, smem],
        out_specs=smem,
        name="plan",
    )(me, picks)


def select_kernel(t, local_blocks, parts, count, after, table_ref, own_ref, *refs):
    came = (refs[:count], refs[count : 2 * count])
    refs = refs[2 * count + after :]
    outs = refs[:2]
    buf, sems = refs[2:]
    for way in range(2):
        code = table_ref[2 * t + way]

        @pl.when(code < local_blocks)
        def _():
            pltpu.make_async_copy(own_ref.at[pl.ds(code * parts, parts)], buf.at[way], sems.at[way]).start()

        for slot in range(count):

            @pl.when(code == local_blocks + slot)
            def _():
                pltpu.make_async_copy(came[way][slot], buf.at[way], sems.at[way]).start()

    for way in range(2):
        pltpu.make_async_copy(own_ref.at[pl.ds(0, parts)], buf.at[way], sems.at[way]).wait()
        pltpu.make_async_copy(buf.at[way], outs[way], sems.at[way]).start()
    for way in range(2):
        pltpu.make_async_copy(buf.at[way], outs[way], sems.at[way]).wait()


def select(t, local_blocks, parts, table, own, came_up, came_down, after):
    count = len(came_up)
    any_spec = pl.BlockSpec(memory_space=ANY)
    shape = jax.ShapeDtypeStruct((parts,) + own.shape[1:], own.dtype)
    return pl.pallas_call(
        functools.partial(select_kernel, t, local_blocks, parts, count, len(after)),
        out_shape=(shape, shape),
        in_specs=[pl.BlockSpec(memory_space=pltpu.SMEM)] + [any_spec] * (1 + 2 * count + len(after)),
        out_specs=(any_spec, any_spec),
        scratch_shapes=[pltpu.VMEM((2,) + shape.shape, shape.dtype), pltpu.SemaphoreType.DMA((2,))],
        compiler_params=pltpu.CompilerParams(vmem_limit_bytes=4 << 20),
        cost_estimate=pl.CostEstimate(flops=0, bytes_accessed=4 << 20, transcendentals=0),
        name="select",
    )(table, own, *came_up, *came_down, *after)


def attend_kernel(low, high, local_blocks, parts, count, chained, table_ref, q_ref, own_ref, *refs):
    came = (refs[:count], refs[count : 2 * count])
    refs = refs[2 * count + (1 if chained else 0) :]
    out_ref, q_buf, kv_buf, o_buf, in_sems, out_sems = refs
    _, pick, ready, _, _ = plan_layout(local_blocks)
    rows = q_ref.shape[1]
    width = q_ref.shape[2]
    heads_here = width // HD
    scale = math.log2(math.e) / math.sqrt(HD)
    slots = RSEL + 1

    def due(block):
        late = table_ref[ready + block]
        return (late > low) & (late <= high) if low >= 0 else late <= high

    def own_part(block):
        return own_ref.at[pl.ds(block * parts, parts)]

    def fetch(block, _):
        @pl.when(due(block))
        def _():
            pltpu.make_async_copy(q_ref.at[pl.ds(block * parts, parts)], q_buf.at[block], in_sems.at[block, slots]).start()
            pltpu.make_async_copy(own_part(block), kv_buf.at[block, 0], in_sems.at[block, 0]).start()
            for slot in range(RSEL):
                code = table_ref[pick + block * RSEL + slot]
                target = kv_buf.at[block, 1 + slot]
                sem = in_sems.at[block, 1 + slot]

                @pl.when(code < local_blocks)
                def _():
                    pltpu.make_async_copy(own_part(code), target, sem).start()

                for way in range(2):
                    for step in range(count):

                        @pl.when(code == local_blocks + way * MAX_STEPS + step)
                        def _():
                            pltpu.make_async_copy(came[way][step], target, sem).start()

        return 0

    def tile(block, part, head):
        cols = pl.ds(pl.multiple_of(head * HD, HD), HD)
        q = q_buf[block, part, :, cols]
        scores = []
        for slot in range(slots):
            for half in range(parts):
                k = kv_buf[block, slot, half, 0, :, cols]
                scores.append(lax.dot_general(q, k, (((1,), (1,)), ((), ())), preferred_element_type=jnp.float32))
        top = functools.reduce(jnp.maximum, [jnp.max(s, axis=1, keepdims=True) for s in scores])
        total = jnp.zeros((rows, HD), jnp.float32)
        mass = jnp.zeros((rows, 1), jnp.float32)
        for index, s in enumerate(scores):
            v = kv_buf[block, index // parts, index % parts, 1, :, cols]
            w = jnp.exp2((s - top) * scale)
            mass = mass + jnp.sum(w, axis=1, keepdims=True)
            total = total + jnp.dot(w.astype(jnp.bfloat16), v, preferred_element_type=jnp.float32)
        o_buf[block, part, :, cols] = (total / mass).astype(jnp.bfloat16)

    def one(block, _):
        @pl.when(due(block))
        def _():
            pltpu.make_async_copy(q_ref.at[pl.ds(0, parts)], q_buf.at[block], in_sems.at[block, slots]).wait()
            for slot in range(slots):
                pltpu.make_async_copy(own_part(0), kv_buf.at[block, slot], in_sems.at[block, slot]).wait()

            def at(i, _):
                tile(block, i // heads_here, i % heads_here)
                return 0

            lax.fori_loop(0, parts * heads_here, at, 0)
            pltpu.make_async_copy(o_buf.at[block], out_ref.at[pl.ds(block * parts, parts)], out_sems.at[block]).start()

        return 0

    def flush(block, _):
        @pl.when(due(block))
        def _():
            pltpu.make_async_copy(o_buf.at[block], out_ref.at[pl.ds(block * parts, parts)], out_sems.at[block]).wait()

        return 0

    lax.fori_loop(0, local_blocks, fetch, 0)
    lax.fori_loop(0, local_blocks, one, 0)
    lax.fori_loop(0, local_blocks, flush, 0)


def attend(low, high, local_blocks, parts, table, q, own, came_up, came_down, so_far):
    count = len(came_up)
    any_spec = pl.BlockSpec(memory_space=ANY)
    chained = so_far is not None
    kv_shape = own.shape[1:]
    inputs = [table, q, own, *came_up, *came_down] + ([so_far] if chained else [])
    return pl.pallas_call(
        functools.partial(attend_kernel, low, high, local_blocks, parts, count, chained),
        out_shape=jax.ShapeDtypeStruct(q.shape, q.dtype),
        in_specs=[pl.BlockSpec(memory_space=pltpu.SMEM)] + [any_spec] * (len(inputs) - 1),
        out_specs=any_spec,
        scratch_shapes=[
            pltpu.VMEM((local_blocks, parts) + q.shape[1:], q.dtype),
            pltpu.VMEM((local_blocks, RSEL + 1, parts) + kv_shape, q.dtype),
            pltpu.VMEM((local_blocks, parts) + q.shape[1:], q.dtype),
            pltpu.SemaphoreType.DMA((local_blocks, RSEL + 2)),
            pltpu.SemaphoreType.DMA((local_blocks,)),
        ],
        input_output_aliases={len(inputs) - 1: 0} if chained else {},
        compiler_params=pltpu.CompilerParams(vmem_limit_bytes=18 << 20),
        cost_estimate=pl.CostEstimate(flops=1 << 30, bytes_accessed=8 << 20, transcendentals=1 << 21),
        name="attend",
    )(*inputs)


def shift(x, by, groups):
    pairs = [(i, i + by) for i in range(groups) if 0 <= i + by < groups]
    return lax.ppermute(x, "ctx", pairs)


def pack_kernel(head_count, *refs):
    ins, out = refs[:-1], refs[-1]
    cols = out.shape[-1]
    for i, ref in enumerate(ins):
        for g in range(head_count):
            out[g, i] = ref[:, g * cols : (g + 1) * cols]


def pack(head_count, *arrays):
    rows, width = arrays[0].shape
    cols = width // head_count
    pieces = 4
    some = rows // pieces
    return pl.pallas_call(
        functools.partial(pack_kernel, head_count),
        grid=(pieces,),
        out_shape=jax.ShapeDtypeStruct((head_count, len(arrays), rows, cols), arrays[0].dtype),
        in_specs=[pl.BlockSpec((some, width), lambda r: (r, 0))] * len(arrays),
        out_specs=pl.BlockSpec((head_count, len(arrays), some, cols), lambda r: (0, 0, r, 0)),
        name="pack",
    )(*arrays)


def swap(x):
    return lax.all_to_all(x, "head", split_axis=0, concat_axis=0, tiled=True)


def hops(steps, groups, local_blocks, parts, q_mine, own, table):
    came_up, came_down = [], []
    q = swap(q_mine)
    out, done = None, -1

    def attend_to(high):
        return attend(done, high, local_blocks, parts, table, q, own, came_up[:high], came_down[:high], out)

    for t in range(steps):
        known = max(0, t + 1 - LATENCY)
        after = [q] if t == LATENCY + 2 else []
        up, down = select(t, local_blocks, parts, table, own, came_up[:known], came_down[:known], after)
        came_up.append(shift(up, 1, groups))
        came_down.append(shift(down, -1, groups))
    for high in (steps - 1, steps):
        out, done = attend_to(high), high
    return swap(out)


def local(queries, keys, values, picks):
    head_count = lax.axis_size("head")
    groups = lax.axis_size("ctx")
    tok_rows, model = queries.shape
    local_blocks = tok_rows * head_count // BLOCK
    parts = BLOCK // tok_rows
    own = swap(pack(head_count, keys, values))
    q_mine = pack(head_count, queries)[:, 0]
    if groups * local_blocks > 16:
        out = by_queries(q_mine, own, picks, groups, local_blocks)
    else:
        table = make_plan(picks, groups, local_blocks)
        order = [MAX_STEPS] + list(range(MIN_STEPS, MAX_STEPS))
        branches = [functools.partial(hops, n, groups, local_blocks, parts) for n in order]
        branches.append(lambda q, kv, tab: by_queries(q, kv, picks, groups, local_blocks))
        steps = table[plan_layout(local_blocks)[3]]
        which = jnp.where(steps == MAX_STEPS, 0, jnp.clip(steps - MIN_STEPS + 1, 1, len(order)))
        out = lax.switch(which, branches, q_mine, own, table)
    return out.transpose(1, 0, 2).reshape(tok_rows, model)


def block_pair(query_block, key_block, value_block):
    scores = jnp.einsum("qhd,khd->hqk", query_block, key_block, preferred_element_type=jnp.float32)
    scores = scores * (1.0 / math.sqrt(HD))
    row_max = jnp.max(scores, axis=-1)
    exponent = jnp.exp(scores - row_max[..., None])
    row_sum = jnp.sum(exponent, axis=-1)
    partial_out = jnp.einsum(
        "hqk,khd->qhd", exponent.astype(jnp.bfloat16), value_block, preferred_element_type=jnp.float32
    )
    return partial_out, row_max, row_sum


def route_tables(picks, local_blocks, ctx_count):
    slots = local_blocks * RSEL
    owners = (picks // local_blocks).reshape(ctx_count, slots)
    within = (picks % local_blocks).reshape(ctx_count, slots)
    owner_ids = jnp.arange(ctx_count, dtype=jnp.int32)
    one_hot = (owners[:, :, None] == owner_ids[None, None, :]).astype(jnp.int32)
    running = jnp.cumsum(one_hot, axis=1)
    position = jnp.sum(one_hot * running, axis=-1) - 1
    return owners, within, position


def by_queries(q_mine, own, picks, ctx_count, local_blocks):
    head_count, tok_rows, width = q_mine.shape
    heads_here = width // HD
    my_index = lax.axis_index("ctx")
    shape = (local_blocks, BLOCK, heads_here, HD)
    q_blocks = swap(q_mine).reshape(shape)
    k_blocks = own[:, 0].reshape(shape)
    v_blocks = own[:, 1].reshape(shape)
    capacity = (local_blocks * RSEL + ctx_count - 1) // ctx_count + 1
    slots = local_blocks * RSEL
    owners, within, position = route_tables(picks, local_blocks, ctx_count)
    mine_owner = lax.dynamic_index_in_dim(owners, my_index, 0, keepdims=False)
    mine_pos = lax.dynamic_index_in_dim(position, my_index, 0, keepdims=False)
    slot_ids = jnp.arange(capacity, dtype=jnp.int32)
    asked = (owners == my_index)[:, :, None] & (position[:, :, None] == slot_ids[None, None, :])
    wanted = jnp.sum(asked.astype(jnp.int32) * within[:, :, None], axis=1)
    pick_back = mine_owner * capacity + mine_pos
    own_out, own_max, own_sum = lax.map(lambda b: block_pair(*b), (q_blocks, k_blocks, v_blocks))
    owner_ids = jnp.arange(ctx_count, dtype=jnp.int32)
    chosen = (mine_owner[:, None, None] == owner_ids[None, :, None]) & (
        mine_pos[:, None, None] == slot_ids[None, None, :]
    )
    query_of_slot = jnp.arange(slots, dtype=jnp.int32) // RSEL
    source_block = jnp.sum(chosen.astype(jnp.int32) * query_of_slot[:, None, None], axis=0)
    arrived = lax.all_to_all(q_blocks[source_block], "ctx", split_axis=0, concat_axis=0, tiled=True)

    def owner_pair(items):
        query_block, block_index = items
        return block_pair(query_block, k_blocks[block_index], v_blocks[block_index])

    far = lax.map(owner_pair, (arrived.reshape((-1,) + shape[1:]), wanted.reshape(-1)))
    back = [
        lax.all_to_all(x.reshape((ctx_count, capacity) + x.shape[1:]), "ctx", split_axis=0, concat_axis=0, tiled=True)
        for x in far
    ]
    back = [x.reshape((-1,) + x.shape[2:])[pick_back] for x in back]
    far_out, far_max, far_sum = [x.reshape((local_blocks, RSEL) + x.shape[1:]) for x in back]
    overall = jnp.maximum(own_max, jnp.max(far_max, axis=1))
    own_factor = jnp.exp(own_max - overall)
    far_factor = jnp.exp(far_max - overall[:, None])
    numer = own_out * jnp.transpose(own_factor, (0, 2, 1))[..., None]
    numer = numer + jnp.sum(far_out * jnp.transpose(far_factor, (0, 1, 3, 2))[..., None], axis=1)
    denom = own_sum * own_factor + jnp.sum(far_sum * far_factor, axis=1)
    result = (numer / jnp.transpose(denom, (0, 2, 1))[..., None]).astype(jnp.bfloat16)
    return swap(result.reshape(head_count, tok_rows, width))


def solution(mesh):
    placed = (P(("ctx", "head"), None), P(("ctx", "head"), None), P(("ctx", "head"), None), P())
    return jax.shard_map(
        local, mesh=mesh, in_specs=placed, out_specs=P(("ctx", "head"), None), check_vma=False
    )
```

```python
import functools
import math

import jax
import jax.numpy as jnp
from jax import lax
from jax.experimental import pallas as pl
from jax.experimental.pallas import tpu as pltpu
from jax.sharding import PartitionSpec as P

HEADS = 16
HD = 128
BLOCK = 512
RSEL = 2
MAX_STEPS = 8
MIN_STEPS = 6
LATENCY = 2
ANY = pl.ANY


def plan_layout(local_blocks):
    send = 0
    pick = 2 * MAX_STEPS
    ready = pick + local_blocks * RSEL
    steps = ready + local_blocks
    return send, pick, ready, steps, steps + 1


def plan_kernel(groups, local_blocks, me_ref, picks_ref, out_ref):
    rows = max(8, 2 * groups)
    blocks = groups * local_blocks
    lanes = 128 * ((blocks + 127) // 128)
    send, pick, ready, steps, _ = plan_layout(local_blocks)
    f32 = jnp.float32
    lane_i = lax.broadcasted_iota(jnp.int32, (rows, lanes), 1)
    row_i = lax.broadcasted_iota(jnp.int32, (rows, lanes), 0)
    lane = lane_i.astype(f32)
    row = row_i.astype(f32)
    back = row >= groups
    place = jnp.where(back, row - groups, row)
    owner = jnp.zeros((rows, lanes), f32)
    for g in range(1, groups):
        owner = owner + jnp.where(lane_i >= g * local_blocks, 1.0, 0.0)
    origin = jnp.where(back, groups - 1 - owner, owner)
    far = jnp.full((rows, lanes), -1.0, f32)
    for entry in range(blocks * RSEL):
        query = entry // RSEL
        group = query // local_blocks
        named = picks_ref[query, entry % RSEL]
        target = jnp.where(back, f32(groups - 1 - group), f32(group))
        far = jnp.where(lane_i == named, jnp.maximum(far, target), far)
    never = f32(1e6)
    crosses = (far > place) & (origin <= place) & (row_i < 2 * groups)
    rank = (far * groups + (groups - 1 - origin)) * lanes + (lanes - 1 - lane)

    def step(t, carry):
        since, sent, came = carry
        now = t.astype(f32)
        able = crosses & (since <= now) & (sent < 0)
        key = jnp.where(able, rank, -1.0)
        best = jnp.max(key, axis=1, keepdims=True)
        goes = jnp.where(able & (key == best), 1.0, 0.0)
        sent = jnp.where(goes > 0, now, sent)
        lands = pltpu.roll(goes, 1, 0)
        came = jnp.where(lands > 0, now, came)
        since = jnp.where(lands > 0, now + LATENCY, since)
        return since, sent, came

    none = jnp.full((rows, lanes), -1.0, f32)
    held = place == origin
    since, sent, came = lax.fori_loop(0, MAX_STEPS, step, (jnp.where(held, 0.0, never), none, none))
    left = jnp.max(jnp.where(crosses & (sent < 0), 1.0, 0.0))
    last = jnp.max(sent)
    out_ref[steps] = jnp.where(left > 0, MAX_STEPS + 1, last.astype(jnp.int32) + 1)
    me = me_ref[0]
    for way in range(2):
        mine = row_i == (me if way == 0 else 2 * groups - 1 - me)
        source = jnp.where(held, lane - owner * local_blocks, came + local_blocks)
        for t in range(MAX_STEPS):
            code = jnp.sum(jnp.where(mine & (sent == t), source, 0.0))
            out_ref[send + 2 * t + way] = code.astype(jnp.int32)
    for block in range(local_blocks):
        late = jnp.int32(0)
        for slot in range(RSEL):
            named = picks_ref[me * local_blocks + block, slot]
            first = me * local_blocks
            below = named < first
            here = (named >= first) & (named < first + local_blocks)
            watched = jnp.where(below, me, 2 * groups - 1 - me)
            came_at = jnp.sum(jnp.where((row_i == watched) & (lane_i == named), came, 0.0)).astype(jnp.int32)
            code = jnp.where(here, named - first, came_at + local_blocks + jnp.where(below, 0, MAX_STEPS))
            out_ref[pick + block * RSEL + slot] = code
            late = jnp.maximum(late, jnp.where(here, 0, came_at + 1))
        out_ref[ready + block] = late


def make_plan(picks, groups, local_blocks):
    size = plan_layout(local_blocks)[-1]
    me = lax.axis_index("ctx").astype(jnp.int32).reshape(1)
    smem = pl.BlockSpec(memory_space=pltpu.SMEM)
    return pl.pallas_call(
        functools.partial(plan_kernel, groups, local_blocks),
        out_shape=jax.ShapeDtypeStruct((size,), jnp.int32),
        in_specs=[smem, smem],
        out_specs=smem,
        name="plan",
    )(me, picks)


def select_kernel(t, local_blocks, parts, count, after, table_ref, own_ref, *refs):
    came = (refs[:count], refs[count : 2 * count])
    refs = refs[2 * count + after :]
    outs = refs[:2]
    buf, sems = refs[2:]
    for way in range(2):
        code = table_ref[2 * t + way]

        @pl.when(code < local_blocks)
        def _():
            pltpu.make_async_copy(own_ref.at[pl.ds(code * parts, parts)], buf.at[way], sems.at[way]).start()

        for slot in range(count):

            @pl.when(code == local_blocks + slot)
            def _():
                pltpu.make_async_copy(came[way][slot], buf.at[way], sems.at[way]).start()

    for way in range(2):
        pltpu.make_async_copy(own_ref.at[pl.ds(0, parts)], buf.at[way], sems.at[way]).wait()
        pltpu.make_async_copy(buf.at[way], outs[way], sems.at[way]).start()
    for way in range(2):
        pltpu.make_async_copy(buf.at[way], outs[way], sems.at[way]).wait()


def select(t, local_blocks, parts, table, own, came_up, came_down, after):
    count = len(came_up)
    any_spec = pl.BlockSpec(memory_space=ANY)
    shape = jax.ShapeDtypeStruct((parts,) + own.shape[1:], own.dtype)
    return pl.pallas_call(
        functools.partial(select_kernel, t, local_blocks, parts, count, len(after)),
        out_shape=(shape, shape),
        in_specs=[pl.BlockSpec(memory_space=pltpu.SMEM)] + [any_spec] * (1 + 2 * count + len(after)),
        out_specs=(any_spec, any_spec),
        scratch_shapes=[pltpu.VMEM((2,) + shape.shape, shape.dtype), pltpu.SemaphoreType.DMA((2,))],
        compiler_params=pltpu.CompilerParams(vmem_limit_bytes=4 << 20),
        cost_estimate=pl.CostEstimate(flops=0, bytes_accessed=4 << 20, transcendentals=0),
        name="select",
    )(table, own, *came_up, *came_down, *after)


def attend_kernel(low, high, local_blocks, parts, count, chained, table_ref, q_ref, own_ref, *refs):
    came = (refs[:count], refs[count : 2 * count])
    refs = refs[2 * count + (1 if chained else 0) :]
    out_ref, q_buf, kv_buf, o_buf, in_sems, out_sems = refs
    _, pick, ready, _, _ = plan_layout(local_blocks)
    rows = q_ref.shape[1]
    width = q_ref.shape[2]
    heads_here = width // HD
    scale = math.log2(math.e) / math.sqrt(HD)
    slots = RSEL + 1

    def due(block):
        late = table_ref[ready + block]
        return (late > low) & (late <= high) if low >= 0 else late <= high

    def own_part(block):
        return own_ref.at[pl.ds(block * parts, parts)]

    def fetch(block, _):
        @pl.when(due(block))
        def _():
            pltpu.make_async_copy(q_ref.at[pl.ds(block * parts, parts)], q_buf.at[block], in_sems.at[block, slots]).start()
            pltpu.make_async_copy(own_part(block), kv_buf.at[block, 0], in_sems.at[block, 0]).start()
            for slot in range(RSEL):
                code = table_ref[pick + block * RSEL + slot]
                target = kv_buf.at[block, 1 + slot]
                sem = in_sems.at[block, 1 + slot]

                @pl.when(code < local_blocks)
                def _():
                    pltpu.make_async_copy(own_part(code), target, sem).start()

                for way in range(2):
                    for step in range(count):

                        @pl.when(code == local_blocks + way * MAX_STEPS + step)
                        def _():
                            pltpu.make_async_copy(came[way][step], target, sem).start()

        return 0

    def tile(block, part, head):
        cols = pl.ds(pl.multiple_of(head * HD, HD), HD)
        q = q_buf[block, part, :, cols]
        scores = []
        for slot in range(slots):
            for half in range(parts):
                k = kv_buf[block, slot, half, 0, :, cols]
                scores.append(lax.dot_general(q, k, (((1,), (1,)), ((), ())), preferred_element_type=jnp.float32))
        top = functools.reduce(jnp.maximum, [jnp.max(s, axis=1, keepdims=True) for s in scores])
        total = jnp.zeros((rows, HD), jnp.float32)
        mass = jnp.zeros((rows, 1), jnp.float32)
        for index, s in enumerate(scores):
            v = kv_buf[block, index // parts, index % parts, 1, :, cols]
            w = jnp.exp2((s - top) * scale)
            mass = mass + jnp.sum(w, axis=1, keepdims=True)
            total = total + jnp.dot(w.astype(jnp.bfloat16), v, preferred_element_type=jnp.float32)
        o_buf[block, part, :, cols] = (total / mass).astype(jnp.bfloat16)

    def one(block, _):
        @pl.when(due(block))
        def _():
            pltpu.make_async_copy(q_ref.at[pl.ds(0, parts)], q_buf.at[block], in_sems.at[block, slots]).wait()
            for slot in range(slots):
                pltpu.make_async_copy(own_part(0), kv_buf.at[block, slot], in_sems.at[block, slot]).wait()

            def at(i, _):
                tile(block, i // heads_here, i % heads_here)
                return 0

            lax.fori_loop(0, parts * heads_here, at, 0)
            pltpu.make_async_copy(o_buf.at[block], out_ref.at[pl.ds(block * parts, parts)], out_sems.at[block]).start()

        return 0

    def flush(block, _):
        @pl.when(due(block))
        def _():
            pltpu.make_async_copy(o_buf.at[block], out_ref.at[pl.ds(block * parts, parts)], out_sems.at[block]).wait()

        return 0

    lax.fori_loop(0, local_blocks, fetch, 0)
    lax.fori_loop(0, local_blocks, one, 0)
    lax.fori_loop(0, local_blocks, flush, 0)


def attend(low, high, local_blocks, parts, table, q, own, came_up, came_down, so_far):
    count = len(came_up)
    any_spec = pl.BlockSpec(memory_space=ANY)
    chained = so_far is not None
    kv_shape = own.shape[1:]
    inputs = [table, q, own, *came_up, *came_down] + ([so_far] if chained else [])
    return pl.pallas_call(
        functools.partial(attend_kernel, low, high, local_blocks, parts, count, chained),
        out_shape=jax.ShapeDtypeStruct(q.shape, q.dtype),
        in_specs=[pl.BlockSpec(memory_space=pltpu.SMEM)] + [any_spec] * (len(inputs) - 1),
        out_specs=any_spec,
        scratch_shapes=[
            pltpu.VMEM((local_blocks, parts) + q.shape[1:], q.dtype),
            pltpu.VMEM((local_blocks, RSEL + 1, parts) + kv_shape, q.dtype),
            pltpu.VMEM((local_blocks, parts) + q.shape[1:], q.dtype),
            pltpu.SemaphoreType.DMA((local_blocks, RSEL + 2)),
            pltpu.SemaphoreType.DMA((local_blocks,)),
        ],
        input_output_aliases={len(inputs) - 1: 0} if chained else {},
        compiler_params=pltpu.CompilerParams(vmem_limit_bytes=18 << 20),
        cost_estimate=pl.CostEstimate(flops=1 << 30, bytes_accessed=8 << 20, transcendentals=1 << 21),
        name="attend",
    )(*inputs)


def shift(x, by, groups):
    pairs = [(i, i + by) for i in range(groups) if 0 <= i + by < groups]
    return lax.ppermute(x, "ctx", pairs)


def pack_kernel(head_count, *refs):
    ins, out = refs[:-1], refs[-1]
    cols = out.shape[-1]
    for i, ref in enumerate(ins):
        for g in range(head_count):
            out[g, i] = ref[:, g * cols : (g + 1) * cols]


def pack(head_count, *arrays):
    rows, width = arrays[0].shape
    cols = width // head_count
    pieces = 4
    some = rows // pieces
    return pl.pallas_call(
        functools.partial(pack_kernel, head_count),
        grid=(pieces,),
        out_shape=jax.ShapeDtypeStruct((head_count, len(arrays), rows, cols), arrays[0].dtype),
        in_specs=[pl.BlockSpec((some, width), lambda r: (r, 0))] * len(arrays),
        out_specs=pl.BlockSpec((head_count, len(arrays), some, cols), lambda r: (0, 0, r, 0)),
        name="pack",
    )(*arrays)


def swap(x):
    return lax.all_to_all(x, "head", split_axis=0, concat_axis=0, tiled=True)


def hops(steps, groups, local_blocks, parts, q_mine, own, table):
    came_up, came_down = [], []
    q = swap(q_mine)
    out, done = None, -1

    def attend_to(high):
        return attend(done, high, local_blocks, parts, table, q, own, came_up[:high], came_down[:high], out)

    for t in range(steps):
        known = max(0, t + 1 - LATENCY)
        after = [q] if t == LATENCY + 2 else []
        up, down = select(t, local_blocks, parts, table, own, came_up[:known], came_down[:known], after)
        came_up.append(shift(up, 1, groups))
        came_down.append(shift(down, -1, groups))
    for high in (steps - 3, steps - 1, steps):
        out, done = attend_to(high), high
    return swap(out)


def local(queries, keys, values, picks):
    head_count = lax.axis_size("head")
    groups = lax.axis_size("ctx")
    tok_rows, model = queries.shape
    local_blocks = tok_rows * head_count // BLOCK
    parts = BLOCK // tok_rows
    own = swap(pack(head_count, keys, values))
    q_mine = pack(head_count, queries)[:, 0]
    if groups * local_blocks > 16:
        out = by_queries(q_mine, own, picks, groups, local_blocks)
    else:
        table = make_plan(picks, groups, local_blocks)
        order = [MAX_STEPS] + list(range(MIN_STEPS, MAX_STEPS))
        branches = [functools.partial(hops, n, groups, local_blocks, parts) for n in order]
        branches.append(lambda q, kv, tab: by_queries(q, kv, picks, groups, local_blocks))
        steps = table[plan_layout(local_blocks)[3]]
        which = jnp.where(steps == MAX_STEPS, 0, jnp.clip(steps - MIN_STEPS + 1, 1, len(order)))
        out = lax.switch(which, branches, q_mine, own, table)
    return out.transpose(1, 0, 2).reshape(tok_rows, model)


def block_pair(query_block, key_block, value_block):
    scores = jnp.einsum("qhd,khd->hqk", query_block, key_block, preferred_element_type=jnp.float32)
    scores = scores * (1.0 / math.sqrt(HD))
    row_max = jnp.max(scores, axis=-1)
    exponent = jnp.exp(scores - row_max[..., None])
    row_sum = jnp.sum(exponent, axis=-1)
    partial_out = jnp.einsum(
        "hqk,khd->qhd", exponent.astype(jnp.bfloat16), value_block, preferred_element_type=jnp.float32
    )
    return partial_out, row_max, row_sum


def route_tables(picks, local_blocks, ctx_count):
    slots = local_blocks * RSEL
    owners = (picks // local_blocks).reshape(ctx_count, slots)
    within = (picks % local_blocks).reshape(ctx_count, slots)
    owner_ids = jnp.arange(ctx_count, dtype=jnp.int32)
    one_hot = (owners[:, :, None] == owner_ids[None, None, :]).astype(jnp.int32)
    running = jnp.cumsum(one_hot, axis=1)
    position = jnp.sum(one_hot * running, axis=-1) - 1
    return owners, within, position


def by_queries(q_mine, own, picks, ctx_count, local_blocks):
    head_count, tok_rows, width = q_mine.shape
    heads_here = width // HD
    my_index = lax.axis_index("ctx")
    shape = (local_blocks, BLOCK, heads_here, HD)
    q_blocks = swap(q_mine).reshape(shape)
    k_blocks = own[:, 0].reshape(shape)
    v_blocks = own[:, 1].reshape(shape)
    capacity = (local_blocks * RSEL + ctx_count - 1) // ctx_count + 1
    slots = local_blocks * RSEL
    owners, within, position = route_tables(picks, local_blocks, ctx_count)
    mine_owner = lax.dynamic_index_in_dim(owners, my_index, 0, keepdims=False)
    mine_pos = lax.dynamic_index_in_dim(position, my_index, 0, keepdims=False)
    slot_ids = jnp.arange(capacity, dtype=jnp.int32)
    asked = (owners == my_index)[:, :, None] & (position[:, :, None] == slot_ids[None, None, :])
    wanted = jnp.sum(asked.astype(jnp.int32) * within[:, :, None], axis=1)
    pick_back = mine_owner * capacity + mine_pos
    own_out, own_max, own_sum = lax.map(lambda b: block_pair(*b), (q_blocks, k_blocks, v_blocks))
    owner_ids = jnp.arange(ctx_count, dtype=jnp.int32)
    chosen = (mine_owner[:, None, None] == owner_ids[None, :, None]) & (
        mine_pos[:, None, None] == slot_ids[None, None, :]
    )
    query_of_slot = jnp.arange(slots, dtype=jnp.int32) // RSEL
    source_block = jnp.sum(chosen.astype(jnp.int32) * query_of_slot[:, None, None], axis=0)
    arrived = lax.all_to_all(q_blocks[source_block], "ctx", split_axis=0, concat_axis=0, tiled=True)

    def owner_pair(items):
        query_block, block_index = items
        return block_pair(query_block, k_blocks[block_index], v_blocks[block_index])

    far = lax.map(owner_pair, (arrived.reshape((-1,) + shape[1:]), wanted.reshape(-1)))
    back = [
        lax.all_to_all(x.reshape((ctx_count, capacity) + x.shape[1:]), "ctx", split_axis=0, concat_axis=0, tiled=True)
        for x in far
    ]
    back = [x.reshape((-1,) + x.shape[2:])[pick_back] for x in back]
    far_out, far_max, far_sum = [x.reshape((local_blocks, RSEL) + x.shape[1:]) for x in back]
    overall = jnp.maximum(own_max, jnp.max(far_max, axis=1))
    own_factor = jnp.exp(own_max - overall)
    far_factor = jnp.exp(far_max - overall[:, None])
    numer = own_out * jnp.transpose(own_factor, (0, 2, 1))[..., None]
    numer = numer + jnp.sum(far_out * jnp.transpose(far_factor, (0, 1, 3, 2))[..., None], axis=1)
    denom = own_sum * own_factor + jnp.sum(far_sum * far_factor, axis=1)
    result = (numer / jnp.transpose(denom, (0, 2, 1))[..., None]).astype(jnp.bfloat16)
    return swap(result.reshape(head_count, tok_rows, width))


def solution(mesh):
    placed = (P(("ctx", "head"), None), P(("ctx", "head"), None), P(("ctx", "head"), None), P())
    return jax.shard_map(
        local, mesh=mesh, in_specs=placed, out_specs=P(("ctx", "head"), None), check_vma=False
    )
```

```python
import functools
import math

import jax
import jax.numpy as jnp
from jax import lax
from jax.experimental import pallas as pl
from jax.experimental.pallas import tpu as pltpu
from jax.sharding import PartitionSpec as P

HEADS = 16
HD = 128
BLOCK = 512
RSEL = 2
MAX_STEPS = 8
MIN_STEPS = 6
LATENCY = 2
ANY = pl.ANY


def plan_layout(local_blocks):
    send = 0
    pick = 2 * MAX_STEPS
    ready = pick + local_blocks * RSEL
    steps = ready + local_blocks
    return send, pick, ready, steps, steps + 1


def plan_kernel(groups, local_blocks, me_ref, picks_ref, out_ref):
    rows = max(8, 2 * groups)
    blocks = groups * local_blocks
    lanes = 128 * ((blocks + 127) // 128)
    send, pick, ready, steps, _ = plan_layout(local_blocks)
    f32 = jnp.float32
    lane_i = lax.broadcasted_iota(jnp.int32, (rows, lanes), 1)
    row_i = lax.broadcasted_iota(jnp.int32, (rows, lanes), 0)
    lane = lane_i.astype(f32)
    row = row_i.astype(f32)
    back = row >= groups
    place = jnp.where(back, row - groups, row)
    owner = jnp.zeros((rows, lanes), f32)
    for g in range(1, groups):
        owner = owner + jnp.where(lane_i >= g * local_blocks, 1.0, 0.0)
    origin = jnp.where(back, groups - 1 - owner, owner)
    far = jnp.full((rows, lanes), -1.0, f32)
    for entry in range(blocks * RSEL):
        query = entry // RSEL
        group = query // local_blocks
        named = picks_ref[query, entry % RSEL]
        target = jnp.where(back, f32(groups - 1 - group), f32(group))
        far = jnp.where(lane_i == named, jnp.maximum(far, target), far)
    never = f32(1e6)
    crosses = (far > place) & (origin <= place) & (row_i < 2 * groups)
    rank = (far * groups + (groups - 1 - origin)) * lanes + (lanes - 1 - lane)

    def step(t, carry):
        since, sent, came = carry
        now = t.astype(f32)
        able = crosses & (since <= now) & (sent < 0)
        key = jnp.where(able, rank, -1.0)
        best = jnp.max(key, axis=1, keepdims=True)
        goes = jnp.where(able & (key == best), 1.0, 0.0)
        sent = jnp.where(goes > 0, now, sent)
        lands = pltpu.roll(goes, 1, 0)
        came = jnp.where(lands > 0, now, came)
        since = jnp.where(lands > 0, now + LATENCY, since)
        return since, sent, came

    none = jnp.full((rows, lanes), -1.0, f32)
    held = place == origin
    since, sent, came = lax.fori_loop(0, MAX_STEPS, step, (jnp.where(held, 0.0, never), none, none))
    left = jnp.max(jnp.where(crosses & (sent < 0), 1.0, 0.0))
    last = jnp.max(sent)
    out_ref[steps] = jnp.where(left > 0, MAX_STEPS + 1, last.astype(jnp.int32) + 1)
    me = me_ref[0]
    for way in range(2):
        mine = row_i == (me if way == 0 else 2 * groups - 1 - me)
        source = jnp.where(held, lane - owner * local_blocks, came + local_blocks)
        for t in range(MAX_STEPS):
            code = jnp.sum(jnp.where(mine & (sent == t), source, 0.0))
            out_ref[send + 2 * t + way] = code.astype(jnp.int32)
    for block in range(local_blocks):
        late = jnp.int32(0)
        for slot in range(RSEL):
            named = picks_ref[me * local_blocks + block, slot]
            first = me * local_blocks
            below = named < first
            here = (named >= first) & (named < first + local_blocks)
            watched = jnp.where(below, me, 2 * groups - 1 - me)
            came_at = jnp.sum(jnp.where((row_i == watched) & (lane_i == named), came, 0.0)).astype(jnp.int32)
            code = jnp.where(here, named - first, came_at + local_blocks + jnp.where(below, 0, MAX_STEPS))
            out_ref[pick + block * RSEL + slot] = code
            late = jnp.maximum(late, jnp.where(here, 0, came_at + 1))
        out_ref[ready + block] = late


def make_plan(picks, groups, local_blocks):
    size = plan_layout(local_blocks)[-1]
    me = lax.axis_index("ctx").astype(jnp.int32).reshape(1)
    smem = pl.BlockSpec(memory_space=pltpu.SMEM)
    return pl.pallas_call(
        functools.partial(plan_kernel, groups, local_blocks),
        out_shape=jax.ShapeDtypeStruct((size,), jnp.int32),
        in_specs=[smem, smem],
        out_specs=smem,
        name="plan",
    )(me, picks)


def select_kernel(t, local_blocks, parts, count, after, table_ref, own_ref, *refs):
    came = (refs[:count], refs[count : 2 * count])
    refs = refs[2 * count + after :]
    outs = refs[:2]
    buf, sems = refs[2:]
    for way in range(2):
        code = table_ref[2 * t + way]

        @pl.when(code < local_blocks)
        def _():
            pltpu.make_async_copy(own_ref.at[pl.ds(code * parts, parts)], buf.at[way], sems.at[way]).start()

        for slot in range(count):

            @pl.when(code == local_blocks + slot)
            def _():
                pltpu.make_async_copy(came[way][slot], buf.at[way], sems.at[way]).start()

    for way in range(2):
        pltpu.make_async_copy(own_ref.at[pl.ds(0, parts)], buf.at[way], sems.at[way]).wait()
        pltpu.make_async_copy(buf.at[way], outs[way], sems.at[way]).start()
    for way in range(2):
        pltpu.make_async_copy(buf.at[way], outs[way], sems.at[way]).wait()


def select(t, local_blocks, parts, table, own, came_up, came_down, after):
    count = len(came_up)
    any_spec = pl.BlockSpec(memory_space=ANY)
    shape = jax.ShapeDtypeStruct((parts,) + own.shape[1:], own.dtype)
    return pl.pallas_call(
        functools.partial(select_kernel, t, local_blocks, parts, count, len(after)),
        out_shape=(shape, shape),
        in_specs=[pl.BlockSpec(memory_space=pltpu.SMEM)] + [any_spec] * (1 + 2 * count + len(after)),
        out_specs=(any_spec, any_spec),
        scratch_shapes=[pltpu.VMEM((2,) + shape.shape, shape.dtype), pltpu.SemaphoreType.DMA((2,))],
        compiler_params=pltpu.CompilerParams(vmem_limit_bytes=4 << 20),
        cost_estimate=pl.CostEstimate(flops=0, bytes_accessed=4 << 20, transcendentals=0),
        name="select",
    )(table, own, *came_up, *came_down, *after)


def attend_kernel(low, high, local_blocks, parts, count, chained, table_ref, q_ref, own_ref, *refs):
    came = (refs[:count], refs[count : 2 * count])
    refs = refs[2 * count + (1 if chained else 0) :]
    out_ref, q_buf, kv_buf, o_buf, in_sems, out_sems = refs
    _, pick, ready, _, _ = plan_layout(local_blocks)
    rows = q_ref.shape[1]
    width = q_ref.shape[2]
    heads_here = width // HD
    scale = math.log2(math.e) / math.sqrt(HD)
    slots = RSEL + 1

    def due(block):
        late = table_ref[ready + block]
        return (late > low) & (late <= high) if low >= 0 else late <= high

    def own_part(block):
        return own_ref.at[pl.ds(block * parts, parts)]

    def fetch(block, _):
        @pl.when(due(block))
        def _():
            pltpu.make_async_copy(q_ref.at[pl.ds(block * parts, parts)], q_buf.at[block], in_sems.at[block, slots]).start()
            pltpu.make_async_copy(own_part(block), kv_buf.at[block, 0], in_sems.at[block, 0]).start()
            for slot in range(RSEL):
                code = table_ref[pick + block * RSEL + slot]
                target = kv_buf.at[block, 1 + slot]
                sem = in_sems.at[block, 1 + slot]

                @pl.when(code < local_blocks)
                def _():
                    pltpu.make_async_copy(own_part(code), target, sem).start()

                for way in range(2):
                    for step in range(count):

                        @pl.when(code == local_blocks + way * MAX_STEPS + step)
                        def _():
                            pltpu.make_async_copy(came[way][step], target, sem).start()

        return 0

    def tile(block, part, head):
        cols = pl.ds(pl.multiple_of(head * HD, HD), HD)
        q = q_buf[block, part, :, cols]
        scores = []
        for slot in range(slots):
            for half in range(parts):
                k = kv_buf[block, slot, half, 0, :, cols]
                scores.append(lax.dot_general(q, k, (((1,), (1,)), ((), ())), preferred_element_type=jnp.float32))
        top = functools.reduce(jnp.maximum, [jnp.max(s, axis=1, keepdims=True) for s in scores])
        total = jnp.zeros((rows, HD), jnp.float32)
        mass = jnp.zeros((rows, 1), jnp.float32)
        for index, s in enumerate(scores):
            v = kv_buf[block, index // parts, index % parts, 1, :, cols]
            w = jnp.exp2((s - top) * scale)
            mass = mass + jnp.sum(w, axis=1, keepdims=True)
            total = total + jnp.dot(w.astype(jnp.bfloat16), v, preferred_element_type=jnp.float32)
        o_buf[block, part, :, cols] = (total / mass).astype(jnp.bfloat16)

    def one(block, _):
        @pl.when(due(block))
        def _():
            pltpu.make_async_copy(q_ref.at[pl.ds(0, parts)], q_buf.at[block], in_sems.at[block, slots]).wait()
            for slot in range(slots):
                pltpu.make_async_copy(own_part(0), kv_buf.at[block, slot], in_sems.at[block, slot]).wait()

            def at(i, _):
                tile(block, i // heads_here, i % heads_here)
                return 0

            lax.fori_loop(0, parts * heads_here, at, 0)
            pltpu.make_async_copy(o_buf.at[block], out_ref.at[pl.ds(block * parts, parts)], out_sems.at[block]).start()

        return 0

    def flush(block, _):
        @pl.when(due(block))
        def _():
            pltpu.make_async_copy(o_buf.at[block], out_ref.at[pl.ds(block * parts, parts)], out_sems.at[block]).wait()

        return 0

    lax.fori_loop(0, local_blocks, fetch, 0)
    lax.fori_loop(0, local_blocks, one, 0)
    lax.fori_loop(0, local_blocks, flush, 0)


def attend(low, high, local_blocks, parts, table, q, own, came_up, came_down, so_far):
    count = len(came_up)
    any_spec = pl.BlockSpec(memory_space=ANY)
    chained = so_far is not None
    kv_shape = own.shape[1:]
    inputs = [table, q, own, *came_up, *came_down] + ([so_far] if chained else [])
    return pl.pallas_call(
        functools.partial(attend_kernel, low, high, local_blocks, parts, count, chained),
        out_shape=jax.ShapeDtypeStruct(q.shape, q.dtype),
        in_specs=[pl.BlockSpec(memory_space=pltpu.SMEM)] + [any_spec] * (len(inputs) - 1),
        out_specs=any_spec,
        scratch_shapes=[
            pltpu.VMEM((local_blocks, parts) + q.shape[1:], q.dtype),
            pltpu.VMEM((local_blocks, RSEL + 1, parts) + kv_shape, q.dtype),
            pltpu.VMEM((local_blocks, parts) + q.shape[1:], q.dtype),
            pltpu.SemaphoreType.DMA((local_blocks, RSEL + 2)),
            pltpu.SemaphoreType.DMA((local_blocks,)),
        ],
        input_output_aliases={len(inputs) - 1: 0} if chained else {},
        compiler_params=pltpu.CompilerParams(vmem_limit_bytes=18 << 20),
        cost_estimate=pl.CostEstimate(flops=1 << 30, bytes_accessed=8 << 20, transcendentals=1 << 21),
        name="attend",
    )(*inputs)


def shift(x, by, groups):
    pairs = [(i, i + by) for i in range(groups) if 0 <= i + by < groups]
    return lax.ppermute(x, "ctx", pairs)


def pack_kernel(head_count, *refs):
    ins, (out, buf, in_sems, out_sems) = refs[:-4], refs[-4:]
    cols = out.shape[-1]

    def come(g, i):
        return pltpu.make_async_copy(ins[i].at[:, pl.ds(g * cols, cols)], buf.at[g, i], in_sems.at[g, i])

    def go(g):
        return pltpu.make_async_copy(buf.at[g], out.at[g], out_sems.at[g])

    for g in range(head_count):
        for i in range(len(ins)):
            come(g, i).start()
    for g in range(head_count):
        for i in range(len(ins)):
            come(g, i).wait()
        go(g).start()
    for g in range(head_count):
        go(g).wait()


def pack(head_count, *arrays):
    rows, width = arrays[0].shape
    shape = (head_count, len(arrays), rows, width // head_count)
    any_spec = pl.BlockSpec(memory_space=ANY)
    return pl.pallas_call(
        functools.partial(pack_kernel, head_count),
        out_shape=jax.ShapeDtypeStruct(shape, arrays[0].dtype),
        in_specs=[any_spec] * len(arrays),
        out_specs=any_spec,
        scratch_shapes=[
            pltpu.VMEM(shape, arrays[0].dtype),
            pltpu.SemaphoreType.DMA((head_count, len(arrays))),
            pltpu.SemaphoreType.DMA((head_count,)),
        ],
        compiler_params=pltpu.CompilerParams(vmem_limit_bytes=8 << 20),
        name="pack",
    )(*arrays)


def swap(x):
    return lax.all_to_all(x, "head", split_axis=0, concat_axis=0, tiled=True)


def hops(steps, groups, local_blocks, parts, q_mine, own, table):
    came_up, came_down = [], []
    q = swap(q_mine)
    out, done = None, -1

    def attend_to(high):
        return attend(done, high, local_blocks, parts, table, q, own, came_up[:high], came_down[:high], out)

    for t in range(steps):
        known = max(0, t + 1 - LATENCY)
        after = [q] if t == LATENCY + 2 else []
        up, down = select(t, local_blocks, parts, table, own, came_up[:known], came_down[:known], after)
        came_up.append(shift(up, 1, groups))
        came_down.append(shift(down, -1, groups))
    for high in (steps - 3, steps - 1, steps):
        out, done = attend_to(high), high
    return swap(out)


def local(queries, keys, values, picks):
    head_count = lax.axis_size("head")
    groups = lax.axis_size("ctx")
    tok_rows, model = queries.shape
    local_blocks = tok_rows * head_count // BLOCK
    parts = BLOCK // tok_rows
    own = swap(pack(head_count, keys, values))
    q_mine = pack(head_count, queries)[:, 0]
    if groups * local_blocks > 16:
        out = by_queries(q_mine, own, picks, groups, local_blocks)
    else:
        table = make_plan(picks, groups, local_blocks)
        order = [MAX_STEPS] + list(range(MIN_STEPS, MAX_STEPS))
        branches = [functools.partial(hops, n, groups, local_blocks, parts) for n in order]
        branches.append(lambda q, kv, tab: by_queries(q, kv, picks, groups, local_blocks))
        steps = table[plan_layout(local_blocks)[3]]
        which = jnp.where(steps == MAX_STEPS, 0, jnp.clip(steps - MIN_STEPS + 1, 1, len(order)))
        out = lax.switch(which, branches, q_mine, own, table)
    return out.transpose(1, 0, 2).reshape(tok_rows, model)


def block_pair(query_block, key_block, value_block):
    scores = jnp.einsum("qhd,khd->hqk", query_block, key_block, preferred_element_type=jnp.float32)
    scores = scores * (1.0 / math.sqrt(HD))
    row_max = jnp.max(scores, axis=-1)
    exponent = jnp.exp(scores - row_max[..., None])
    row_sum = jnp.sum(exponent, axis=-1)
    partial_out = jnp.einsum(
        "hqk,khd->qhd", exponent.astype(jnp.bfloat16), value_block, preferred_element_type=jnp.float32
    )
    return partial_out, row_max, row_sum


def route_tables(picks, local_blocks, ctx_count):
    slots = local_blocks * RSEL
    owners = (picks // local_blocks).reshape(ctx_count, slots)
    within = (picks % local_blocks).reshape(ctx_count, slots)
    owner_ids = jnp.arange(ctx_count, dtype=jnp.int32)
    one_hot = (owners[:, :, None] == owner_ids[None, None, :]).astype(jnp.int32)
    running = jnp.cumsum(one_hot, axis=1)
    position = jnp.sum(one_hot * running, axis=-1) - 1
    return owners, within, position


def by_queries(q_mine, own, picks, ctx_count, local_blocks):
    head_count, tok_rows, width = q_mine.shape
    heads_here = width // HD
    my_index = lax.axis_index("ctx")
    shape = (local_blocks, BLOCK, heads_here, HD)
    q_blocks = swap(q_mine).reshape(shape)
    k_blocks = own[:, 0].reshape(shape)
    v_blocks = own[:, 1].reshape(shape)
    capacity = (local_blocks * RSEL + ctx_count - 1) // ctx_count + 1
    slots = local_blocks * RSEL
    owners, within, position = route_tables(picks, local_blocks, ctx_count)
    mine_owner = lax.dynamic_index_in_dim(owners, my_index, 0, keepdims=False)
    mine_pos = lax.dynamic_index_in_dim(position, my_index, 0, keepdims=False)
    slot_ids = jnp.arange(capacity, dtype=jnp.int32)
    asked = (owners == my_index)[:, :, None] & (position[:, :, None] == slot_ids[None, None, :])
    wanted = jnp.sum(asked.astype(jnp.int32) * within[:, :, None], axis=1)
    pick_back = mine_owner * capacity + mine_pos
    own_out, own_max, own_sum = lax.map(lambda b: block_pair(*b), (q_blocks, k_blocks, v_blocks))
    owner_ids = jnp.arange(ctx_count, dtype=jnp.int32)
    chosen = (mine_owner[:, None, None] == owner_ids[None, :, None]) & (
        mine_pos[:, None, None] == slot_ids[None, None, :]
    )
    query_of_slot = jnp.arange(slots, dtype=jnp.int32) // RSEL
    source_block = jnp.sum(chosen.astype(jnp.int32) * query_of_slot[:, None, None], axis=0)
    arrived = lax.all_to_all(q_blocks[source_block], "ctx", split_axis=0, concat_axis=0, tiled=True)

    def owner_pair(items):
        query_block, block_index = items
        return block_pair(query_block, k_blocks[block_index], v_blocks[block_index])

    far = lax.map(owner_pair, (arrived.reshape((-1,) + shape[1:]), wanted.reshape(-1)))
    back = [
        lax.all_to_all(x.reshape((ctx_count, capacity) + x.shape[1:]), "ctx", split_axis=0, concat_axis=0, tiled=True)
        for x in far
    ]
    back = [x.reshape((-1,) + x.shape[2:])[pick_back] for x in back]
    far_out, far_max, far_sum = [x.reshape((local_blocks, RSEL) + x.shape[1:]) for x in back]
    overall = jnp.maximum(own_max, jnp.max(far_max, axis=1))
    own_factor = jnp.exp(own_max - overall)
    far_factor = jnp.exp(far_max - overall[:, None])
    numer = own_out * jnp.transpose(own_factor, (0, 2, 1))[..., None]
    numer = numer + jnp.sum(far_out * jnp.transpose(far_factor, (0, 1, 3, 2))[..., None], axis=1)
    denom = own_sum * own_factor + jnp.sum(far_sum * far_factor, axis=1)
    result = (numer / jnp.transpose(denom, (0, 2, 1))[..., None]).astype(jnp.bfloat16)
    return swap(result.reshape(head_count, tok_rows, width))


def solution(mesh):
    placed = (P(("ctx", "head"), None), P(("ctx", "head"), None), P(("ctx", "head"), None), P())
    return jax.shard_map(
        local, mesh=mesh, in_specs=placed, out_specs=P(("ctx", "head"), None), check_vma=False
    )
```

```python
import functools
import math

import jax
import jax.numpy as jnp
from jax import lax
from jax.experimental import pallas as pl
from jax.experimental.pallas import tpu as pltpu
from jax.sharding import PartitionSpec as P

HEADS = 16
HD = 128
BLOCK = 512
RSEL = 2
MAX_STEPS = 8
MIN_STEPS = 6
LATENCY = 2
ANY = pl.ANY


def plan_layout(local_blocks):
    send = 0
    pick = 2 * MAX_STEPS
    ready = pick + local_blocks * RSEL
    steps = ready + local_blocks
    return send, pick, ready, steps, steps + 1


def plan_kernel(groups, local_blocks, me_ref, picks_ref, out_ref):
    rows = max(8, 2 * groups)
    blocks = groups * local_blocks
    lanes = 128 * ((blocks + 127) // 128)
    send, pick, ready, steps, _ = plan_layout(local_blocks)
    f32 = jnp.float32
    lane_i = lax.broadcasted_iota(jnp.int32, (rows, lanes), 1)
    row_i = lax.broadcasted_iota(jnp.int32, (rows, lanes), 0)
    lane = lane_i.astype(f32)
    row = row_i.astype(f32)
    back = row >= groups
    place = jnp.where(back, row - groups, row)
    owner = jnp.zeros((rows, lanes), f32)
    for g in range(1, groups):
        owner = owner + jnp.where(lane_i >= g * local_blocks, 1.0, 0.0)
    origin = jnp.where(back, groups - 1 - owner, owner)
    far = jnp.full((rows, lanes), -1.0, f32)
    for entry in range(blocks * RSEL):
        query = entry // RSEL
        group = query // local_blocks
        named = picks_ref[query, entry % RSEL]
        target = jnp.where(back, f32(groups - 1 - group), f32(group))
        far = jnp.where(lane_i == named, jnp.maximum(far, target), far)
    never = f32(1e6)
    crosses = (far > place) & (origin <= place) & (row_i < 2 * groups)
    rank = (far * groups + (groups - 1 - origin)) * lanes + (lanes - 1 - lane)

    def step(t, carry):
        since, sent, came = carry
        now = t.astype(f32)
        able = crosses & (since <= now) & (sent < 0)
        key = jnp.where(able, rank, -1.0)
        best = jnp.max(key, axis=1, keepdims=True)
        goes = jnp.where(able & (key == best), 1.0, 0.0)
        sent = jnp.where(goes > 0, now, sent)
        lands = pltpu.roll(goes, 1, 0)
        came = jnp.where(lands > 0, now, came)
        since = jnp.where(lands > 0, now + LATENCY, since)
        return since, sent, came

    none = jnp.full((rows, lanes), -1.0, f32)
    held = place == origin
    since, sent, came = lax.fori_loop(0, MAX_STEPS, step, (jnp.where(held, 0.0, never), none, none))
    left = jnp.max(jnp.where(crosses & (sent < 0), 1.0, 0.0))
    last = jnp.max(sent)
    out_ref[steps] = jnp.where(left > 0, MAX_STEPS + 1, last.astype(jnp.int32) + 1)
    me = me_ref[0]
    for way in range(2):
        mine = row_i == (me if way == 0 else 2 * groups - 1 - me)
        source = jnp.where(held, lane - owner * local_blocks, came + local_blocks)
        for t in range(MAX_STEPS):
            code = jnp.sum(jnp.where(mine & (sent == t), source, 0.0))
            out_ref[send + 2 * t + way] = code.astype(jnp.int32)
    for block in range(local_blocks):
        late = jnp.int32(0)
        for slot in range(RSEL):
            named = picks_ref[me * local_blocks + block, slot]
            first = me * local_blocks
            below = named < first
            here = (named >= first) & (named < first + local_blocks)
            watched = jnp.where(below, me, 2 * groups - 1 - me)
            came_at = jnp.sum(jnp.where((row_i == watched) & (lane_i == named), came, 0.0)).astype(jnp.int32)
            code = jnp.where(here, named - first, came_at + local_blocks + jnp.where(below, 0, MAX_STEPS))
            out_ref[pick + block * RSEL + slot] = code
            late = jnp.maximum(late, jnp.where(here, 0, came_at + 1))
        out_ref[ready + block] = late


def make_plan(picks, groups, local_blocks):
    size = plan_layout(local_blocks)[-1]
    me = lax.axis_index("ctx").astype(jnp.int32).reshape(1)
    smem = pl.BlockSpec(memory_space=pltpu.SMEM)
    return pl.pallas_call(
        functools.partial(plan_kernel, groups, local_blocks),
        out_shape=jax.ShapeDtypeStruct((size,), jnp.int32),
        in_specs=[smem, smem],
        out_specs=smem,
        name="plan",
    )(me, picks)


def select_kernel(t, local_blocks, parts, count, after, table_ref, own_ref, *refs):
    came = (refs[:count], refs[count : 2 * count])
    refs = refs[2 * count + after :]
    outs = refs[:2]
    buf, sems = refs[2:]
    for way in range(2):
        code = table_ref[2 * t + way]

        @pl.when(code < local_blocks)
        def _():
            pltpu.make_async_copy(own_ref.at[pl.ds(code * parts, parts)], buf.at[way], sems.at[way]).start()

        for slot in range(count):

            @pl.when(code == local_blocks + slot)
            def _():
                pltpu.make_async_copy(came[way][slot], buf.at[way], sems.at[way]).start()

    for way in range(2):
        pltpu.make_async_copy(own_ref.at[pl.ds(0, parts)], buf.at[way], sems.at[way]).wait()
        pltpu.make_async_copy(buf.at[way], outs[way], sems.at[way]).start()
    for way in range(2):
        pltpu.make_async_copy(buf.at[way], outs[way], sems.at[way]).wait()


def select(t, local_blocks, parts, table, own, came_up, came_down, after):
    count = len(came_up)
    any_spec = pl.BlockSpec(memory_space=ANY)
    shape = jax.ShapeDtypeStruct((parts,) + own.shape[1:], own.dtype)
    return pl.pallas_call(
        functools.partial(select_kernel, t, local_blocks, parts, count, len(after)),
        out_shape=(shape, shape),
        in_specs=[pl.BlockSpec(memory_space=pltpu.SMEM)] + [any_spec] * (1 + 2 * count + len(after)),
        out_specs=(any_spec, any_spec),
        scratch_shapes=[pltpu.VMEM((2,) + shape.shape, shape.dtype), pltpu.SemaphoreType.DMA((2,))],
        compiler_params=pltpu.CompilerParams(vmem_limit_bytes=4 << 20),
        cost_estimate=pl.CostEstimate(flops=0, bytes_accessed=4 << 20, transcendentals=0),
        name="select",
    )(table, own, *came_up, *came_down, *after)


def attend_kernel(low, high, local_blocks, parts, count, chained, table_ref, q_ref, own_ref, *refs):
    came = (refs[:count], refs[count : 2 * count])
    refs = refs[2 * count + (1 if chained else 0) :]
    out_ref, q_buf, kv_buf, o_buf, in_sems, out_sems = refs
    _, pick, ready, _, _ = plan_layout(local_blocks)
    rows = q_ref.shape[1]
    width = q_ref.shape[2]
    heads_here = width // HD
    scale = math.log2(math.e) / math.sqrt(HD)
    slots = RSEL + 1

    def due(block):
        late = table_ref[ready + block]
        return (late > low) & (late <= high) if low >= 0 else late <= high

    def own_part(block):
        return own_ref.at[pl.ds(block * parts, parts)]

    def fetch(block, _):
        @pl.when(due(block))
        def _():
            pltpu.make_async_copy(q_ref.at[pl.ds(block * parts, parts)], q_buf.at[block], in_sems.at[block, slots]).start()
            pltpu.make_async_copy(own_part(block), kv_buf.at[block, 0], in_sems.at[block, 0]).start()
            for slot in range(RSEL):
                code = table_ref[pick + block * RSEL + slot]
                target = kv_buf.at[block, 1 + slot]
                sem = in_sems.at[block, 1 + slot]

                @pl.when(code < local_blocks)
                def _():
                    pltpu.make_async_copy(own_part(code), target, sem).start()

                for way in range(2):
                    for step in range(count):

                        @pl.when(code == local_blocks + way * MAX_STEPS + step)
                        def _():
                            pltpu.make_async_copy(came[way][step], target, sem).start()

        return 0

    def tile(block, part, head):
        cols = pl.ds(pl.multiple_of(head * HD, HD), HD)
        q = q_buf[block, part, :, cols]
        scores = []
        for slot in range(slots):
            for half in range(parts):
                k = kv_buf[block, slot, half, 0, :, cols]
                scores.append(lax.dot_general(q, k, (((1,), (1,)), ((), ())), preferred_element_type=jnp.float32))
        top = functools.reduce(jnp.maximum, [jnp.max(s, axis=1, keepdims=True) for s in scores])
        total = jnp.zeros((rows, HD), jnp.float32)
        mass = jnp.zeros((rows, 1), jnp.float32)
        for index, s in enumerate(scores):
            v = kv_buf[block, index // parts, index % parts, 1, :, cols]
            w = jnp.exp2((s - top) * scale)
            mass = mass + jnp.sum(w, axis=1, keepdims=True)
            total = total + jnp.dot(w.astype(jnp.bfloat16), v, preferred_element_type=jnp.float32)
        o_buf[block, part, :, cols] = (total / mass).astype(jnp.bfloat16)

    def one(block, _):
        @pl.when(due(block))
        def _():
            pltpu.make_async_copy(q_ref.at[pl.ds(0, parts)], q_buf.at[block], in_sems.at[block, slots]).wait()
            for slot in range(slots):
                pltpu.make_async_copy(own_part(0), kv_buf.at[block, slot], in_sems.at[block, slot]).wait()

            def at(i, _):
                tile(block, i // heads_here, i % heads_here)
                return 0

            lax.fori_loop(0, parts * heads_here, at, 0)
            pltpu.make_async_copy(o_buf.at[block], out_ref.at[pl.ds(block * parts, parts)], out_sems.at[block]).start()

        return 0

    def flush(block, _):
        @pl.when(due(block))
        def _():
            pltpu.make_async_copy(o_buf.at[block], out_ref.at[pl.ds(block * parts, parts)], out_sems.at[block]).wait()

        return 0

    lax.fori_loop(0, local_blocks, fetch, 0)
    lax.fori_loop(0, local_blocks, one, 0)
    lax.fori_loop(0, local_blocks, flush, 0)


def attend(low, high, local_blocks, parts, table, q, own, came_up, came_down, so_far):
    count = len(came_up)
    any_spec = pl.BlockSpec(memory_space=ANY)
    chained = so_far is not None
    kv_shape = own.shape[1:]
    inputs = [table, q, own, *came_up, *came_down] + ([so_far] if chained else [])
    return pl.pallas_call(
        functools.partial(attend_kernel, low, high, local_blocks, parts, count, chained),
        out_shape=jax.ShapeDtypeStruct(q.shape, q.dtype),
        in_specs=[pl.BlockSpec(memory_space=pltpu.SMEM)] + [any_spec] * (len(inputs) - 1),
        out_specs=any_spec,
        scratch_shapes=[
            pltpu.VMEM((local_blocks, parts) + q.shape[1:], q.dtype),
            pltpu.VMEM((local_blocks, RSEL + 1, parts) + kv_shape, q.dtype),
            pltpu.VMEM((local_blocks, parts) + q.shape[1:], q.dtype),
            pltpu.SemaphoreType.DMA((local_blocks, RSEL + 2)),
            pltpu.SemaphoreType.DMA((local_blocks,)),
        ],
        input_output_aliases={len(inputs) - 1: 0} if chained else {},
        compiler_params=pltpu.CompilerParams(vmem_limit_bytes=18 << 20),
        cost_estimate=pl.CostEstimate(flops=1 << 30, bytes_accessed=8 << 20, transcendentals=1 << 21),
        name="attend",
    )(*inputs)


def shift(x, by, groups):
    pairs = [(i, i + by) for i in range(groups) if 0 <= i + by < groups]
    return lax.ppermute(x, "ctx", pairs)


def pack_kernel(head_count, *refs):
    ins, (out, buf, in_sems, out_sems) = refs[:-4], refs[-4:]
    cols = out.shape[-1]

    def come(g, i):
        return pltpu.make_async_copy(ins[i].at[:, pl.ds(g * cols, cols)], buf.at[g, i], in_sems.at[g, i])

    def go(g):
        return pltpu.make_async_copy(buf.at[g], out.at[g], out_sems.at[g])

    for g in range(head_count):
        for i in range(len(ins)):
            come(g, i).start()
    for g in range(head_count):
        for i in range(len(ins)):
            come(g, i).wait()
        go(g).start()
    for g in range(head_count):
        go(g).wait()


def pack(head_count, *arrays):
    rows, width = arrays[0].shape
    shape = (head_count, len(arrays), rows, width // head_count)
    any_spec = pl.BlockSpec(memory_space=ANY)
    return pl.pallas_call(
        functools.partial(pack_kernel, head_count),
        out_shape=jax.ShapeDtypeStruct(shape, arrays[0].dtype),
        in_specs=[any_spec] * len(arrays),
        out_specs=any_spec,
        scratch_shapes=[
            pltpu.VMEM(shape, arrays[0].dtype),
            pltpu.SemaphoreType.DMA((head_count, len(arrays))),
            pltpu.SemaphoreType.DMA((head_count,)),
        ],
        compiler_params=pltpu.CompilerParams(vmem_limit_bytes=60 << 20),
        name="pack",
    )(*arrays)


def swap(x):
    return lax.all_to_all(x, "head", split_axis=0, concat_axis=0, tiled=True)


def hops(steps, groups, local_blocks, parts, q_mine, own, table):
    came_up, came_down = [], []
    q = swap(q_mine)
    out, done = None, -1

    def attend_to(high):
        return attend(done, high, local_blocks, parts, table, q, own, came_up[:high], came_down[:high], out)

    for t in range(steps):
        known = max(0, t + 1 - LATENCY)
        after = [q] if t == LATENCY + 2 else []
        up, down = select(t, local_blocks, parts, table, own, came_up[:known], came_down[:known], after)
        came_up.append(shift(up, 1, groups))
        came_down.append(shift(down, -1, groups))
    for high in (steps - 3, steps - 1, steps):
        out, done = attend_to(high), high
    return swap(out)


def local(queries, keys, values, picks):
    head_count = lax.axis_size("head")
    groups = lax.axis_size("ctx")
    tok_rows, model = queries.shape
    local_blocks = tok_rows * head_count // BLOCK
    parts = BLOCK // tok_rows
    own = swap(pack(head_count, keys, values))
    q_mine = pack(head_count, queries)[:, 0]
    if groups * local_blocks > 16:
        out = by_queries(q_mine, own, picks, groups, local_blocks)
    else:
        table = make_plan(picks, groups, local_blocks)
        order = [MAX_STEPS] + list(range(MIN_STEPS, MAX_STEPS))
        branches = [functools.partial(hops, n, groups, local_blocks, parts) for n in order]
        branches.append(lambda q, kv, tab: by_queries(q, kv, picks, groups, local_blocks))
        steps = table[plan_layout(local_blocks)[3]]
        which = jnp.where(steps == MAX_STEPS, 0, jnp.clip(steps - MIN_STEPS + 1, 1, len(order)))
        out = lax.switch(which, branches, q_mine, own, table)
    return out.transpose(1, 0, 2).reshape(tok_rows, model)


def block_pair(query_block, key_block, value_block):
    scores = jnp.einsum("qhd,khd->hqk", query_block, key_block, preferred_element_type=jnp.float32)
    scores = scores * (1.0 / math.sqrt(HD))
    row_max = jnp.max(scores, axis=-1)
    exponent = jnp.exp(scores - row_max[..., None])
    row_sum = jnp.sum(exponent, axis=-1)
    partial_out = jnp.einsum(
        "hqk,khd->qhd", exponent.astype(jnp.bfloat16), value_block, preferred_element_type=jnp.float32
    )
    return partial_out, row_max, row_sum


def route_tables(picks, local_blocks, ctx_count):
    slots = local_blocks * RSEL
    owners = (picks // local_blocks).reshape(ctx_count, slots)
    within = (picks % local_blocks).reshape(ctx_count, slots)
    owner_ids = jnp.arange(ctx_count, dtype=jnp.int32)
    one_hot = (owners[:, :, None] == owner_ids[None, None, :]).astype(jnp.int32)
    running = jnp.cumsum(one_hot, axis=1)
    position = jnp.sum(one_hot * running, axis=-1) - 1
    return owners, within, position


def by_queries(q_mine, own, picks, ctx_count, local_blocks):
    head_count, tok_rows, width = q_mine.shape
    heads_here = width // HD
    my_index = lax.axis_index("ctx")
    shape = (local_blocks, BLOCK, heads_here, HD)
    q_blocks = swap(q_mine).reshape(shape)
    k_blocks = own[:, 0].reshape(shape)
    v_blocks = own[:, 1].reshape(shape)
    capacity = (local_blocks * RSEL + ctx_count - 1) // ctx_count + 1
    slots = local_blocks * RSEL
    owners, within, position = route_tables(picks, local_blocks, ctx_count)
    mine_owner = lax.dynamic_index_in_dim(owners, my_index, 0, keepdims=False)
    mine_pos = lax.dynamic_index_in_dim(position, my_index, 0, keepdims=False)
    slot_ids = jnp.arange(capacity, dtype=jnp.int32)
    asked = (owners == my_index)[:, :, None] & (position[:, :, None] == slot_ids[None, None, :])
    wanted = jnp.sum(asked.astype(jnp.int32) * within[:, :, None], axis=1)
    pick_back = mine_owner * capacity + mine_pos
    own_out, own_max, own_sum = lax.map(lambda b: block_pair(*b), (q_blocks, k_blocks, v_blocks))
    owner_ids = jnp.arange(ctx_count, dtype=jnp.int32)
    chosen = (mine_owner[:, None, None] == owner_ids[None, :, None]) & (
        mine_pos[:, None, None] == slot_ids[None, None, :]
    )
    query_of_slot = jnp.arange(slots, dtype=jnp.int32) // RSEL
    source_block = jnp.sum(chosen.astype(jnp.int32) * query_of_slot[:, None, None], axis=0)
    arrived = lax.all_to_all(q_blocks[source_block], "ctx", split_axis=0, concat_axis=0, tiled=True)

    def owner_pair(items):
        query_block, block_index = items
        return block_pair(query_block, k_blocks[block_index], v_blocks[block_index])

    far = lax.map(owner_pair, (arrived.reshape((-1,) + shape[1:]), wanted.reshape(-1)))
    back = [
        lax.all_to_all(x.reshape((ctx_count, capacity) + x.shape[1:]), "ctx", split_axis=0, concat_axis=0, tiled=True)
        for x in far
    ]
    back = [x.reshape((-1,) + x.shape[2:])[pick_back] for x in back]
    far_out, far_max, far_sum = [x.reshape((local_blocks, RSEL) + x.shape[1:]) for x in back]
    overall = jnp.maximum(own_max, jnp.max(far_max, axis=1))
    own_factor = jnp.exp(own_max - overall)
    far_factor = jnp.exp(far_max - overall[:, None])
    numer = own_out * jnp.transpose(own_factor, (0, 2, 1))[..., None]
    numer = numer + jnp.sum(far_out * jnp.transpose(far_factor, (0, 1, 3, 2))[..., None], axis=1)
    denom = own_sum * own_factor + jnp.sum(far_sum * far_factor, axis=1)
    result = (numer / jnp.transpose(denom, (0, 2, 1))[..., None]).astype(jnp.bfloat16)
    return swap(result.reshape(head_count, tok_rows, width))


def solution(mesh):
    placed = (P(("ctx", "head"), None), P(("ctx", "head"), None), P(("ctx", "head"), None), P())
    return jax.shard_map(
        local, mesh=mesh, in_specs=placed, out_specs=P(("ctx", "head"), None), check_vma=False
    )
```
